32 devices in a mesh: context: 8 (over y, x, core), tensor: 4 (over z).
Axes of the slice: x: 2, y: 2, z: 4, core: 2. Of those that a mesh axis runs over, the one named last changes fastest.
Arguments:
- queries: bfloat16 [16384, 8192], P('context', 'tensor'), may hold values from -6 to 6
- key_rows: bfloat16 [16384, 8192], P('context', 'tensor'), may hold values from -6 to 6
- value_rows: bfloat16 [16384, 8192], P('context', 'tensor'), may hold values from -200 to 200
- short_filter: float32 [7, 512], P(None, 'tensor'), may hold values from -2 to 2
- medium_filter: bfloat16 [128, 512], P(None, 'tensor'), may hold values from -0.5 to 0.5
- decays: float32 [512, 16], P('tensor'), may hold values from 0 to 1, as said below
- residue: float32 [512, 16], P('tensor'), may hold values from -1.5 to 1.5
- skip_gain: float32 [8192], P('tensor'), may hold values from -1 to 1
- norm_gain: float32 [8192], P('tensor'), may hold values from 0.5 to 1.5
Outputs:
- mixer_out: bfloat16 [16384, 8192], P('context', 'tensor')
The draws below stay inside these ranges and needn't reach their ends.
Inputs may be any that keep to these rules, and one draw needn't show every extreme that they name: decays lie between 1 / 81920 and 1 / 32.
All inputs are finite; a program needn't handle non-finite values.
Results may differ from the reference program's by a relative error of at most 0.0065.
Values may be sent and summed in bfloat16 or wider, within the bound.
No kernel may reach another device: no remote copies, remote signals or barrier semaphores. Data moves between devices by JAX's collectives and lax.ppermute only.
A program may use at most 192 MiB of HBM per device.

```python
import math
import jax
import jax.numpy as jnp
from jax import lax

D = 8192
GROUP_CH = 16
SE_TAPS = 7
MR_TAPS = 128
MODES = 16
SEQ = 16384
GROUPS = 512


def draw_value_rows(key, part):
    key = jax.random.fold_in(key, 17)
    noise_key, row_key = jax.random.split(key)
    columns = jnp.arange(D, dtype=jnp.float32) / D
    row_scale = 10.0 ** jax.random.uniform(row_key, (SEQ, 1), jnp.float32)
    noise = jnp.clip(jax.random.normal(noise_key, (SEQ, D), jnp.float32), -6.0, 6.0)
    column_scale = 10.0 ** columns
    return (0.3 * noise * row_scale * column_scale[None, :]).astype(jnp.bfloat16)


def draw_decays(key, part):
    key = jax.random.fold_in(key, 29)
    pick_key, slow_key, fast_key = jax.random.split(key, 3)
    shape = (GROUPS, MODES)
    lowest = math.log(0.2 / SEQ)
    middle = math.log(2.0 / SEQ)
    highest = math.log(1.0 / 32.0)
    slow_share = 0.5
    slow = jnp.exp(jax.random.uniform(slow_key, shape, jnp.float32, lowest, middle))
    fast = jnp.exp(jax.random.uniform(fast_key, shape, jnp.float32, middle, highest))
    chosen = jax.random.uniform(pick_key, shape, jnp.float32) < slow_share
    return jnp.where(chosen, slow, fast)


def steps_of(key, extent, shards, smallest, high):
    level, own = 1.0, jax.random.fold_in(key, 6)
    for dim, parts in shards:
        heights = jnp.exp(jax.random.uniform(jax.random.fold_in(own, dim), (parts,), jnp.float32, smallest / len(shards), high / len(shards)))
        level = level * jnp.repeat(heights, extent[dim] // parts).reshape([-1 if axis == dim else 1 for axis in range(len(extent))])
    return level


def scatter_about(key, extent, scale, reach, cuts=(), kind=jnp.bfloat16):
    drawn = jax.random.normal(key, extent, jnp.float32) * scale
    if len(cuts) > 0:
        drawn = steps_of(key, extent, cuts, -0.22, 0.18) * drawn
    return jnp.clip(drawn, min=-reach, max=reach).astype(kind)


def setup_inputs(seed: int = 0) -> dict:
    splits = jax.random.split(jax.random.key(seed), 10)
    queries = scatter_about(splits[0], (SEQ, D), 1.0, 6.0, ((0, 8), (1, 4)))
    key_rows = scatter_about(splits[1], (SEQ, D), 1.0, 6.0, ((0, 8), (1, 4)))
    value_rows = draw_value_rows(jax.random.fold_in(splits[9], 71), 0)
    short_filter = scatter_about(splits[3], (SE_TAPS, GROUPS), SE_TAPS ** -0.5, 2.0, ((1, 4),), jnp.float32)
    medium_filter = scatter_about(splits[4], (MR_TAPS, GROUPS), MR_TAPS ** -0.5, 0.5, ((1, 4),))
    decays = draw_decays(jax.random.fold_in(splits[9], 71), 0)
    residue = scatter_about(splits[6], (GROUPS, MODES), 0.25, 1.5, ((0, 4),), jnp.float32)
    skip_gain = jnp.clip(jax.random.uniform(splits[7], (D,), jnp.float32, -1.0, 1.0) * steps_of(splits[7], (D,), ((0, 4),), -0.4, 0.0), -1.0, 1.0)
    norm_gain = jnp.clip(1.0 + 0.1 * jax.random.normal(splits[8], (D,), jnp.float32), 0.5, 1.5)
    return {"queries": queries, "key_rows": key_rows, "value_rows": value_rows, "short_filter": short_filter, "medium_filter": medium_filter, "decays": decays, "residue": residue, "skip_gain": skip_gain, "norm_gain": norm_gain}


HIGHEST = lax.Precision.HIGHEST

def medium_reference(first, medium_filter):
    width = MR_TAPS
    slab = math.gcd(D, 1024)
    lead = jnp.concatenate([jnp.zeros((width, D), jnp.float32), first.astype(jnp.float32)], axis=0).T
    inner = jnp.arange(2 * width)[:, None]
    outer = jnp.arange(width)[None, :]
    offset = outer + width - inner
    onehot = (offset[:, :, None] == jnp.arange(width)[None, None, :]).astype(jnp.float32)
    toeplitz = jnp.einsum('jit,tg->gji', onehot, medium_filter.astype(jnp.float32), precision=HIGHEST)
    lead = lead.reshape(D // slab, slab // GROUP_CH, GROUP_CH, SEQ // width + 1, width)
    toeplitz = toeplitz.reshape(D // slab, slab // GROUP_CH, 2 * width, width)

    def per_slab(pair):
        blocks, tiles = pair
        windows = jnp.concatenate([blocks[:, :, :-1], blocks[:, :, 1:]], axis=3)
        return jnp.einsum('gkbj,gji->gkbi', windows, tiles, precision=HIGHEST)
    result = lax.map(per_slab, (lead, toeplitz))
    return result.reshape(D, SEQ).T

def long_reference(second, profile):
    slab = math.gcd(D, 1024)
    count = D // slab
    pieces = second.astype(jnp.float32).reshape(SEQ, count, slab).transpose(1, 0, 2)
    kernels = profile.reshape(SEQ, count, slab // GROUP_CH).transpose(1, 0, 2)

    def per_slab(pair):
        piece, kernel = pair
        spread = jnp.repeat(kernel, GROUP_CH, axis=1)
        spectrum = jnp.fft.rfft(piece, n=2 * SEQ, axis=0) * jnp.fft.rfft(spread, n=2 * SEQ, axis=0)
        return jnp.fft.irfft(spectrum, n=2 * SEQ, axis=0)[:SEQ]
    result = lax.map(per_slab, (pieces, kernels))
    return result.transpose(1, 0, 2).reshape(SEQ, D)

def reference(queries, key_rows, value_rows, short_filter, medium_filter, decays, residue, skip_gain, norm_gain):
    gated = key_rows.astype(jnp.float32) * value_rows.astype(jnp.float32)
    spread = jnp.repeat(short_filter, GROUP_CH, axis=1)
    padded = jnp.concatenate([jnp.zeros((SE_TAPS - 1, D), jnp.float32), gated], axis=0)
    short = jnp.zeros((SEQ, D), jnp.float32)
    for delay in range(SE_TAPS):
        begin = SE_TAPS - 1 - delay
        short = short + spread[delay][None, :] * padded[begin:begin + SEQ]
    first = (queries.astype(jnp.float32) * short).astype(jnp.bfloat16)
    medium = medium_reference(first, medium_filter)
    second = (key_rows.astype(jnp.float32) * medium).astype(jnp.bfloat16)
    amplitude = residue * jnp.sqrt(-jnp.expm1(-2.0 * decays))
    times = jnp.arange(SEQ, dtype=jnp.float32)
    profile = jnp.zeros((SEQ, GROUPS), jnp.float32)
    for mode in range(MODES):
        profile = profile + amplitude[:, mode][None, :] * jnp.exp(-decays[:, mode][None, :] * times[:, None])
    conv = long_reference(second, profile).astype(jnp.bfloat16)
    mixed = value_rows.astype(jnp.float32) * (conv.astype(jnp.float32) + skip_gain[None, :] * second.astype(jnp.float32))
    mean_square = lax.optimization_barrier(jnp.mean(mixed * mixed, axis=1))
    scale = lax.rsqrt(mean_square + 1e-06)
    return (mixed * scale[:, None] * norm_gain[None, :]).astype(jnp.bfloat16)
```

```python
import functools

import jax
import jax.numpy as jnp
from jax import lax
from jax.experimental import pallas as pl
from jax.experimental.pallas import tpu as pltpu
from jax.sharding import PartitionSpec as P

GROUP_CH = 16
LANES = 128
PACK = LANES // GROUP_CH
WIDE = 256
F32 = jnp.float32
BF16 = jnp.bfloat16


def split2(value):
    high = value.astype(BF16)
    return high, (value - high.astype(F32)).astype(BF16)


def passed_along(value, axis, steps):
    count = lax.axis_size(axis)
    return lax.ppermute(value, axis, [(source, source + steps) for source in range(count - steps)])


def mix_kernel(q, k, v, halo, short_taps, medium_taps, profile, tail_high, tail_low, lead_high,
               lead_low, block_decay, skip, y_out, state_out, gated, first_t, key_t, y_t, ends):
    rows = q.shape[0]
    modes = tail_high.shape[0] // PACK
    gated[0:8, :] = halo[LANES:LANES + 8, :].astype(F32) + halo[LANES + 8:LANES + 16, :].astype(F32)
    first_t[:, 0:LANES] = halo[0:LANES, :].T
    for begin in range(0, rows, WIDE):
        part = pl.ds(begin, WIDE)
        gated[pl.ds(begin + 8, WIDE), :] = k[part, :].astype(F32) * v[part, :].astype(F32)
    taps = short_taps[...]
    for begin in range(0, rows, WIDE):
        part = pl.ds(begin, WIDE)
        total = taps[0:1, :] * gated[pl.ds(begin + 8, WIDE), :]
        for delay in range(1, 7):
            total = total + taps[delay:delay + 1, :] * gated[pl.ds(begin + 8 - delay, WIDE), :]
        first = (q[part, :].astype(F32) * total).astype(BF16)
        first_t[:, begin + LANES:begin + LANES + WIDE] = first.T
        key_t[:, begin:begin + WIDE] = k[part, :].T
    skip_t = jnp.broadcast_to(skip[...], (LANES, LANES)).T
    row_i = lax.broadcasted_iota(jnp.int32, (LANES, LANES), 0)
    col_i = lax.broadcasted_iota(jnp.int32, (LANES, LANES), 1)
    causal = col_i >= row_i
    zero = jnp.zeros((LANES, LANES), BF16)
    halves = rows // LANES
    blocks = rows // WIDE
    lane = lax.broadcasted_iota(jnp.int32, (rows // WIDE * GROUP_CH, LANES), 1)
    pad = jnp.zeros((LANES - 6 * modes, WIDE), BF16)
    pad_lead = jnp.zeros((LANES - 3 * modes, WIDE), BF16)
    for g in range(PACK):
        chans = pl.ds(g * GROUP_CH, GROUP_CH)
        mode_rows = pl.ds(g * modes, modes)
        turned = pltpu.roll(jnp.broadcast_to(medium_taps[g:g + 1, :].astype(F32), (LANES, LANES)),
                            0, 1, stride=1, stride_axis=0)
        medium_w = jnp.concatenate(
            [jnp.where(causal, 0.0, turned), jnp.where(causal, turned, 0.0)], axis=0).astype(BF16)
        window = jnp.concatenate(
            [first_t[chans, b * LANES:(b + 2) * LANES] for b in range(halves)], axis=0)
        medium = jnp.dot(window, medium_w, preferred_element_type=F32)
        key = jnp.concatenate(
            [key_t[chans, b * LANES:(b + 1) * LANES] for b in range(halves)], axis=0)
        second = (key.astype(F32) * medium).astype(BF16)
        second = jnp.concatenate(
            [jnp.concatenate([second[2 * b * GROUP_CH:(2 * b + 1) * GROUP_CH],
                              second[(2 * b + 1) * GROUP_CH:(2 * b + 2) * GROUP_CH]], axis=1)
             for b in range(blocks)], axis=0)
        tails = jnp.concatenate([tail_high[mode_rows, :]] * 3 + [tail_low[mode_rows, :]] * 3 + [pad], axis=0)
        sums = lax.dot_general(second, tails, (((1,), (1,)), ((), ())), preferred_element_type=F32)
        sums = sums + pltpu.roll(sums, LANES - 3 * modes, 1)
        decay = block_decay[g:g + 1, :]
        state = jnp.zeros((GROUP_CH, LANES), F32)
        states = []
        for b in range(blocks):
            states.append(state)
            state = decay * state + sums[b * GROUP_CH:(b + 1) * GROUP_CH, :]
        ends[chans, :] = state
        high, low = split2(jnp.concatenate(states, axis=0))
        carried = jnp.where((lane >= modes) & (lane < 2 * modes), low, high)
        carried = jnp.where(lane < 3 * modes, carried, jnp.zeros_like(carried))
        leads = jnp.concatenate(
            [lead_high[mode_rows, :], lead_high[mode_rows, :], lead_low[mode_rows, :], pad_lead], axis=0)
        turned = pltpu.roll(jnp.broadcast_to(profile[g:g + 1, :], (LANES, WIDE)), 0, 1, stride=1, stride_axis=0)
        near = jnp.where(causal, turned[:, :LANES], 0.0).astype(BF16)
        long_w = jnp.concatenate(
            [jnp.concatenate([near, turned[:, LANES:].astype(BF16)], axis=1),
             jnp.concatenate([zero, near], axis=1)], axis=0)
        y = jnp.dot(second, long_w, preferred_element_type=F32)
        y = y + jnp.dot(carried, leads, preferred_element_type=F32)
        gain = skip_t[g * GROUP_CH:(g + 1) * GROUP_CH, :]
        gain = jnp.concatenate([jnp.concatenate([gain, gain], axis=1)] * blocks, axis=0)
        y = (y + gain * second.astype(F32)).astype(BF16)
        for b in range(blocks):
            y_t[chans, b * WIDE:(b + 1) * WIDE] = y[b * GROUP_CH:(b + 1) * GROUP_CH, :]
    for begin in range(0, rows, WIDE):
        y_out[pl.ds(begin, WIDE), :] = y_t[:, begin:begin + WIDE].T
    state_out[...] = ends[...].T[:modes, :]


def mix(q, k, v, halo, short_taps, medium_taps, profile, tails, leads, block_decay, skip):
    rows, chans = q.shape
    modes = tails[0].shape[0] * GROUP_CH // chans
    grid = (chans // LANES,)
    column = lambda height: pl.BlockSpec((height, LANES), lambda i: (0, i))
    down = lambda height, width: pl.BlockSpec((height, width), lambda i: (i, 0))
    return pl.pallas_call(
        mix_kernel,
        grid=grid,
        out_shape=(jax.ShapeDtypeStruct((rows, chans), BF16), jax.ShapeDtypeStruct((modes, chans), F32)),
        in_specs=[column(rows)] * 3 + [
            column(halo.shape[0]), column(8), down(PACK, LANES), down(PACK, WIDE),
            down(PACK * modes, WIDE), down(PACK * modes, WIDE), down(PACK * modes, WIDE),
            down(PACK * modes, WIDE), down(PACK, LANES), column(1)],
        out_specs=(column(rows), column(modes)),
        scratch_shapes=[
            pltpu.VMEM((rows + 8, LANES), F32),
            pltpu.VMEM((LANES, rows + LANES), BF16),
            pltpu.VMEM((LANES, rows), BF16),
            pltpu.VMEM((LANES, rows), BF16),
            pltpu.VMEM((LANES, LANES), F32),
        ],
        compiler_params=pltpu.CompilerParams(vmem_limit_bytes=40 << 20),
        cost_estimate=pl.CostEstimate(flops=8 * rows * chans * WIDE, bytes_accessed=8 * rows * chans, transcendentals=0),
        name="mix",
    )(q, k, v, halo, short_taps, medium_taps, profile, *tails, *leads, block_decay, skip)


def join_kernel(y, v, states, weights, decay_row, state_amp, mixed_out, energy_out, energy):
    rows = y.shape[0]
    modes = state_amp.shape[0]
    step = pl.program_id(0)
    count = states.shape[0]
    entry = jnp.zeros((modes, LANES), F32)
    for source in range(count):
        entry = entry + weights[source] * states[source]
    entry = entry * state_amp[...]
    lane = lax.broadcasted_iota(jnp.int32, (modes, LANES), 1) // GROUP_CH
    spread = jnp.concatenate([jnp.where(lane == g, entry, 0.0) for g in range(PACK)], axis=0)
    entry_w = jnp.concatenate(split2(spread), axis=0)
    rate = decay_row[...]
    time = lax.broadcasted_iota(jnp.int32, (LANES, LANES), 0).astype(F32) + 1.0
    lead = jnp.exp(-rate * time)
    fade = jnp.exp(-rate * float(LANES))
    for begin in range(0, rows, LANES):
        part = pl.ds(begin, LANES)
        lead16 = lead.astype(BF16)
        carried = jnp.dot(jnp.concatenate([lead16, lead16], axis=1), entry_w, preferred_element_type=F32)
        mixed = v[part, :].astype(F32) * (y[part, :].astype(F32) + carried)
        mixed_out[part, :] = mixed.astype(BF16)
        square = mixed * mixed

        @pl.when(step == 0)
        def _():
            energy[part, :] = square

        @pl.when(step > 0)
        def _():
            energy[part, :] += square

        lead = lead * fade

    @pl.when(step == pl.num_programs(0) - 1)
    def _():
        for begin in range(0, rows, LANES):
            energy_out[:, begin:begin + LANES] = jnp.sum(energy[pl.ds(begin, LANES), :].T, axis=0, keepdims=True)


def join(y, v, states, weights, decay_row, state_amp):
    rows, chans = y.shape
    count, modes, _ = states.shape
    column = lambda height: pl.BlockSpec((height, LANES), lambda i: (0, i))
    deep = pl.BlockSpec((count, modes, LANES), lambda i: (0, 0, i))
    return pl.pallas_call(
        join_kernel,
        grid=(chans // LANES,),
        out_shape=(jax.ShapeDtypeStruct((rows, chans), BF16), jax.ShapeDtypeStruct((1, rows), F32)),
        in_specs=[column(rows), column(rows), deep, deep, column(1), column(modes)],
        out_specs=(column(rows), pl.BlockSpec((1, rows), lambda i: (0, 0))),
        scratch_shapes=[pltpu.VMEM((rows, LANES), F32)],
        compiler_params=pltpu.CompilerParams(vmem_limit_bytes=40 << 20),
        cost_estimate=pl.CostEstimate(flops=2 * rows * chans * WIDE, bytes_accessed=6 * rows * chans, transcendentals=0),
        name="join",
    )(y, v, states, weights, decay_row, state_amp)


def local(queries, key_rows, value_rows, short_filter, medium_filter, decays, residue, skip_gain,
          norm_gain, width):
    rows, chans = queries.shape
    groups, modes = decays.shape
    taps = short_filter.shape[0]
    short_taps = jnp.pad(jnp.repeat(short_filter, GROUP_CH, axis=1), ((0, 8 - taps), (0, 0)))
    near = rows - LANES
    gated = key_rows[near - 8:].astype(F32) * value_rows[near - 8:].astype(F32)
    total = jnp.zeros((LANES, chans), F32)
    for delay in range(taps):
        total = total + short_taps[delay][None, :] * gated[8 - delay:8 - delay + LANES]
    first = (queries[near:].astype(F32) * total).astype(BF16)
    halo = passed_along(jnp.concatenate([first, *split2(gated[LANES:])], axis=0), "context", 1)

    amplitude = residue * jnp.sqrt(-jnp.expm1(-2.0 * decays))
    time = jnp.arange(WIDE, dtype=F32)
    fade = jnp.exp(-decays[:, :, None] * time[None, None, :])
    profile = jnp.sum(amplitude[:, :, None] * fade, axis=1)
    tails = split2(jnp.exp(-decays[:, :, None] * (WIDE - 1 - time)[None, None, :]).reshape(groups * modes, WIDE))
    leads = split2((amplitude[:, :, None] * jnp.exp(-decays[:, :, None] * (time + 1.0)[None, None, :])).reshape(groups * modes, WIDE))
    block_decay = jnp.pad(jnp.tile(jnp.exp(-decays * WIDE), (1, 3)), ((0, 0), (0, LANES - 3 * modes)))
    y, state = mix(queries, key_rows, value_rows, halo, short_taps, medium_filter.T, profile, tails,
                   leads, block_decay, skip_gain[None, :])
    states = lax.all_gather(state, "context")
    count = lax.axis_size("context")
    gap = (lax.axis_index("context") - 1 - jnp.arange(count)).astype(F32)
    rate = jnp.repeat(decays.T, GROUP_CH, axis=1)
    weights = jnp.where(gap[:, None, None] >= 0.0,
                        jnp.exp(-rate[None] * (jnp.maximum(gap, 0.0) * rows)[:, None, None]), 0.0)
    state_amp = jnp.repeat(amplitude.T, GROUP_CH, axis=1)
    mixed, energy = join(y, value_rows, states, weights, decays.reshape(1, groups * modes), state_amp)
    energy = lax.psum(energy, "tensor")
    scale = lax.rsqrt(energy[0] / width + 1e-06)
    return (mixed.astype(F32) * scale[:, None] * norm_gain[None, :]).astype(BF16)


def solution(mesh):
    def whole(*args):
        return jax.shard_map(
            functools.partial(local, width=args[0].shape[1]),
            mesh=mesh,
            in_specs=(
                P("context", "tensor"),
                P("context", "tensor"),
                P("context", "tensor"),
                P(None, "tensor"),
                P(None, "tensor"),
                P("tensor", None),
                P("tensor", None),
                P("tensor"),
                P("tensor"),
            ),
            out_specs=P("context", "tensor"),
            check_vma=False,
        )(*args)

    return whole
```

```python
import functools
import math

import jax
import jax.numpy as jnp
from jax import lax
from jax.experimental import pallas as pl
from jax.experimental.pallas import tpu as pltpu
from jax.sharding import PartitionSpec as P

GROUP_CH = 16
LANES = 128
PACK = LANES // GROUP_CH
WIDE = 256
MODES = 16
SHORT = 7
RATE, AMP, SKIP = SHORT, SHORT + 1, SHORT + 2
STRIP = 256
JOIN_STRIP = 256
MIX_VMEM = 20 << 20
JOIN_VMEM = 20 << 20
F32 = jnp.float32
BF16 = jnp.bfloat16


def split2(value):
    high = value.astype(BF16)
    return high, (value - high.astype(F32)).astype(BF16)


def passed_along(value, axis, steps):
    count = lax.axis_size(axis)
    return lax.ppermute(value, axis, [(source, source + steps) for source in range(count - steps)])


def edge_kernel(q, k, v, taps, halo_out, gated):
    rows = q.shape[0]
    begin = rows - LANES
    kv = k[begin - 16:, :].astype(F32) * v[begin - 16:, :].astype(F32)
    gated[...] = kv
    total = taps[0:1, :] * gated[16:, :]
    for delay in range(1, SHORT):
        total = total + taps[delay:delay + 1, :] * gated[pl.ds(16 - delay, LANES), :]
    halo_out[0:LANES, :] = (q[begin:, :].astype(F32) * total).astype(BF16)
    last = kv[LANES + 8:, :]
    high = last.astype(BF16).astype(F32)
    halo_out[LANES:LANES + 16, :] = jnp.concatenate([high, last - high], axis=0).astype(BF16)


def edge(q, k, v, params):
    rows, chans = q.shape
    wide = math.gcd(chans, 512)
    tall = math.gcd(rows, 256)
    last = pl.BlockSpec((tall, wide), lambda i: (rows // tall - 1, i))
    column = lambda height: pl.BlockSpec((height, wide), lambda i: (0, i))
    return pl.pallas_call(
        edge_kernel,
        grid=(chans // wide,),
        out_shape=jax.ShapeDtypeStruct((LANES + 16, chans), BF16),
        in_specs=[last] * 3 + [column(params.shape[0])],
        out_specs=column(LANES + 16),
        scratch_shapes=[pltpu.VMEM((LANES + 16, wide), F32)],
        compiler_params=pltpu.CompilerParams(vmem_limit_bytes=16 << 20),
        name="edge",
    )(q, k, v, params)


def mix_kernel(q, k, v, halo, params, medium_taps, y_out, state_out, gated, first_t, key_t, y_t, seconds):
    rows = q.shape[0]
    blocks = rows // WIDE
    row_i = lax.broadcasted_iota(jnp.int32, (LANES, LANES), 0)
    col_i = lax.broadcasted_iota(jnp.int32, (LANES, LANES), 1)
    causal = col_i >= row_i
    zero = jnp.zeros((LANES, LANES), BF16)
    time_down = lax.broadcasted_iota(jnp.int32, (WIDE, LANES), 0).astype(F32)
    time_along = lax.broadcasted_iota(jnp.int32, (LANES, WIDE), 1).astype(F32)
    lane_group = lax.broadcasted_iota(jnp.int32, (WIDE, LANES), 1) // MODES

    def strip(s, nothing):
        here = pl.ds(pl.multiple_of(s * LANES, LANES), LANES)
        taps = params[:, here]
        gated[0:8, :] = halo[LANES:LANES + 8, here].astype(F32) + halo[LANES + 8:LANES + 16, here].astype(F32)
        first_t[:, 0:LANES] = halo[0:LANES, here].T
        for begin in range(0, rows, LANES):
            part = pl.ds(begin, LANES)
            keys = k[part, here]
            fresh = keys.astype(F32) * v[part, here].astype(F32)
            gated[pl.ds(begin + 8, LANES), :] = fresh
            total = taps[0:1, :] * fresh
            for delay in range(1, SHORT):
                total = total + taps[delay:delay + 1, :] * gated[pl.ds(begin + 8 - delay, LANES), :]
            first = (q[part, here].astype(F32) * total).astype(BF16)
            first_t[:, begin + LANES:begin + 2 * LANES] = first.T
            key_t[:, begin:begin + LANES] = keys.T

        for g in range(PACK):
            chans = pl.ds(g * GROUP_CH, GROUP_CH)
            turned = jnp.broadcast_to(medium_taps[pl.ds(s * PACK + g, 1), :], (LANES, LANES))
            turned = pltpu.roll(turned, 0, 1, stride=1, stride_axis=0)
            medium_w = jnp.concatenate(
                [jnp.where(causal, 0.0, turned), jnp.where(causal, turned, 0.0)], axis=0).astype(BF16)
            window = jnp.concatenate(
                [first_t[chans, b * LANES:(b + 2) * LANES] for b in range(rows // LANES)], axis=0)
            medium = jnp.dot(window, medium_w, preferred_element_type=F32)
            key = jnp.concatenate(
                [key_t[chans, b * LANES:(b + 1) * LANES] for b in range(rows // LANES)], axis=0)
            second = (key.astype(F32) * medium).astype(BF16)
            for b in range(rows // LANES):
                seconds[(b // 2) * GROUP_CH:(b // 2 + 1) * GROUP_CH,
                        g * WIDE + (b % 2) * LANES:g * WIDE + (b % 2 + 1) * LANES] = (
                    second[b * GROUP_CH:(b + 1) * GROUP_CH])

        rate = taps[RATE:RATE + 1, :]
        tails = jnp.exp(-rate * (WIDE - 1.0 - time_down)).astype(BF16)
        tails_w = jnp.concatenate([jnp.where(lane_group == g, tails, jnp.zeros_like(tails)) for g in range(PACK)], axis=0)
        sums = jnp.dot(seconds[...], tails_w, preferred_element_type=F32)
        decay = jnp.exp(-rate * float(WIDE))
        state = jnp.zeros((GROUP_CH, LANES), F32)
        states = []
        for b in range(blocks):
            states.append(state)
            state = decay * state + sums[b * GROUP_CH:(b + 1) * GROUP_CH, :]
        state_out[:, here] = state.astype(BF16)
        carried = jnp.concatenate(split2(jnp.concatenate(states, axis=0)), axis=1)

        down = lambda row: jnp.broadcast_to(taps[row:row + 1, :], (LANES, LANES)).T
        rate_t, amp_t, skip_t = down(RATE), down(AMP), down(SKIP)
        both = lambda half: jnp.concatenate([half, half], axis=1)
        power = both(amp_t) * jnp.exp(-both(rate_t) * time_along)
        lead = (power * jnp.exp(-both(rate_t))).astype(BF16)
        for g in range(PACK):
            chans = pl.ds(g * GROUP_CH, GROUP_CH)
            mine = slice(g * MODES, (g + 1) * MODES)
            profile = jnp.sum(power[mine], axis=0, keepdims=True)
            turned = pltpu.roll(jnp.broadcast_to(profile, (LANES, WIDE)), 0, 1, stride=1, stride_axis=0)
            near = jnp.where(causal, turned[:, :LANES], 0.0).astype(BF16)
            pieces = [jnp.concatenate([near, turned[:, LANES:].astype(BF16)], axis=1),
                      jnp.concatenate([zero, near], axis=1)]
            lead_g = [lead[mine]]
            if g > 0:
                lead_g = [jnp.zeros((g * MODES, WIDE), BF16)] + lead_g
            if g < PACK - 1:
                lead_g = lead_g + [jnp.zeros(((PACK - 1 - g) * MODES, WIDE), BF16)]
            second = seconds[:, g * WIDE:(g + 1) * WIDE]
            y = jnp.dot(jnp.concatenate([second, carried], axis=1),
                        jnp.concatenate(pieces + lead_g + lead_g, axis=0), preferred_element_type=F32)
            gain = both(skip_t[g * GROUP_CH:(g + 1) * GROUP_CH, :])
            gain = jnp.concatenate([gain] * blocks, axis=0)
            y = (y + gain * second.astype(F32)).astype(BF16)
            for b in range(blocks):
                y_t[chans, b * WIDE:(b + 1) * WIDE] = y[b * GROUP_CH:(b + 1) * GROUP_CH, :]
        for begin in range(0, rows, LANES):
            y_out[pl.ds(begin, LANES), here] = y_t[:, begin:begin + LANES].T
        return nothing

    lax.fori_loop(0, q.shape[1] // LANES, strip, 0)


def mix(q, k, v, halo, params, medium_taps):
    rows, chans = q.shape
    wide = math.gcd(chans, STRIP)
    column = lambda height: pl.BlockSpec((height, wide), lambda i: (0, i))
    return pl.pallas_call(
        mix_kernel,
        grid=(chans // wide,),
        out_shape=(jax.ShapeDtypeStruct((rows, chans), BF16), jax.ShapeDtypeStruct((GROUP_CH, chans), BF16)),
        in_specs=[column(rows)] * 3 + [column(halo.shape[0]), column(params.shape[0]),
                                       pl.BlockSpec((wide // GROUP_CH, LANES), lambda i: (i, 0))],
        out_specs=(column(rows), column(GROUP_CH)),
        scratch_shapes=[
            pltpu.VMEM((rows + 8, LANES), F32),
            pltpu.VMEM((LANES, rows + LANES), BF16),
            pltpu.VMEM((LANES, rows), BF16),
            pltpu.VMEM((LANES, rows), BF16),
            pltpu.VMEM((LANES, PACK * WIDE), BF16),
        ],
        compiler_params=pltpu.CompilerParams(vmem_limit_bytes=MIX_VMEM),
        cost_estimate=pl.CostEstimate(flops=8 * rows * chans * WIDE, bytes_accessed=8 * rows * chans, transcendentals=0),
        name="mix",
    )(q, k, v, halo, params, medium_taps)


def join_kernel(y, v, states, weights, params, mixed_out, energy_out, energy):
    rows, wide = y.shape
    step = pl.program_id(0)

    @pl.when(step == 0)
    def _():
        energy[...] = jnp.zeros_like(energy)

    row_i = lax.broadcasted_iota(jnp.int32, (LANES, LANES), 0)
    col_i = lax.broadcasted_iota(jnp.int32, (LANES, LANES), 1)
    own = row_i // GROUP_CH == col_i // MODES
    time = row_i.astype(F32) + 1.0
    entry = jnp.zeros((GROUP_CH, wide), F32)
    for source in range(states.shape[0]):
        entry = entry + weights[source:source + 1, :] * states[source].astype(F32)
    entries, leads = [], []
    for s in range(wide // LANES):
        here = slice(s * LANES, (s + 1) * LANES)
        spread = jnp.where(own, jnp.concatenate([entry[:, here]] * PACK, axis=0), 0.0)
        entries.append(jnp.concatenate(split2(spread), axis=1))
        leads.append(jnp.exp(-params[RATE:RATE + 1, here] * time))
    for b in range(rows // LANES):
        part = pl.ds(b * LANES, LANES)
        total = energy[part, :]
        for s in range(wide // LANES):
            here = slice(s * LANES, (s + 1) * LANES)
            lead = (leads[s] * jnp.exp(-params[RATE:RATE + 1, here] * float(b * LANES))).astype(BF16)
            carried = lax.dot_general(jnp.concatenate([lead, lead], axis=1), entries[s],
                                      (((1,), (1,)), ((), ())), preferred_element_type=F32)
            mixed = v[part, here].astype(F32) * (y[part, here].astype(F32) + carried)
            mixed_out[part, here] = mixed.astype(BF16)
            total = total + mixed * mixed
        energy[part, :] = total

    @pl.when(step == pl.num_programs(0) - 1)
    def _():
        for begin in range(0, rows, LANES):
            energy_out[:, begin:begin + LANES] = jnp.sum(energy[pl.ds(begin, LANES), :].T, axis=0, keepdims=True)


def join(y, v, states, weights, params):
    rows, chans = y.shape
    wide = math.gcd(chans, JOIN_STRIP)
    column = lambda height: pl.BlockSpec((height, wide), lambda i: (0, i))
    return pl.pallas_call(
        join_kernel,
        grid=(chans // wide,),
        out_shape=(jax.ShapeDtypeStruct((rows, chans), BF16), jax.ShapeDtypeStruct((1, rows), F32)),
        in_specs=[column(rows), column(rows), pl.BlockSpec((states.shape[0], GROUP_CH, wide), lambda i: (0, 0, i)),
                  column(weights.shape[0]), column(params.shape[0])],
        out_specs=(column(rows), pl.BlockSpec((1, rows), lambda i: (0, 0))),
        scratch_shapes=[pltpu.VMEM((rows, LANES), F32)],
        compiler_params=pltpu.CompilerParams(vmem_limit_bytes=JOIN_VMEM),
        cost_estimate=pl.CostEstimate(flops=2 * rows * chans * WIDE, bytes_accessed=6 * rows * chans, transcendentals=0),
        name="join",
    )(y, v, states, weights, params)


def local(queries, key_rows, value_rows, short_filter, medium_filter, decays, residue, skip_gain,
          norm_gain, width):
    rows, chans = queries.shape
    amplitude = residue * jnp.sqrt(-jnp.expm1(-2.0 * decays))
    params = jnp.concatenate([
        jnp.repeat(short_filter, GROUP_CH, axis=1),
        decays.reshape(1, chans), amplitude.reshape(1, chans), skip_gain[None, :],
        jnp.zeros((16 - SHORT - 3, chans), F32)], axis=0)
    halo = passed_along(edge(queries, key_rows, value_rows, params), "context", 1)
    y, state = mix(queries, key_rows, value_rows, halo, params, medium_filter.T.astype(F32))
    states = lax.all_gather(state, "context")
    count = lax.axis_size("context")
    gap = (lax.axis_index("context") - 1 - jnp.arange(count)).astype(F32)[:, None]
    weights = jnp.where(gap >= 0.0, params[AMP:AMP + 1] * jnp.exp(-params[RATE:RATE + 1] * (jnp.maximum(gap, 0.0) * rows)), 0.0)
    mixed, energy = join(y, value_rows, states, weights, params)
    energy = lax.psum(energy, "tensor")
    scale = lax.rsqrt(energy[0] / width + 1e-06)
    return (mixed.astype(F32) * scale[:, None] * norm_gain[None, :]).astype(BF16)


def solution(mesh):
    def whole(*args):
        return jax.shard_map(
            functools.partial(local, width=args[0].shape[1]),
            mesh=mesh,
            in_specs=(
                P("context", "tensor"),
                P("context", "tensor"),
                P("context", "tensor"),
                P(None, "tensor"),
                P(None, "tensor"),
                P("tensor", None),
                P("tensor", None),
                P("tensor"),
                P("tensor"),
            ),
            out_specs=P("context", "tensor"),
            check_vma=False,
        )(*args)

    return whole
```

```python
import functools
import math

import jax
import jax.numpy as jnp
from jax import lax
from jax.experimental import pallas as pl
from jax.experimental.pallas import tpu as pltpu
from jax.sharding import PartitionSpec as P

GROUP_CH = 16
LANES = 128
PACK = LANES // GROUP_CH
WIDE = 256
MODES = 16
SHORT = 7
RATE, AMP, SKIP = SHORT, SHORT + 1, SHORT + 2
EARLY = 0
JOIN_STRIP = 256
MIX_VMEM = 60 << 20
JOIN_VMEM = 60 << 20
F32 = jnp.float32
BF16 = jnp.bfloat16


def split2(value):
    high = value.astype(BF16)
    return high, (value - high.astype(F32)).astype(BF16)


def passed_along(value, axis, steps):
    count = lax.axis_size(axis)
    return lax.ppermute(value, axis, [(source, source + steps) for source in range(count - steps)])


def edge_kernel(q, k, v, taps, halo_out, gated):
    rows = q.shape[0]
    begin = rows - LANES
    kv = k[begin - 16:, :].astype(F32) * v[begin - 16:, :].astype(F32)
    gated[...] = kv
    total = taps[0:1, :] * gated[16:, :]
    for delay in range(1, SHORT):
        total = total + taps[delay:delay + 1, :] * gated[pl.ds(16 - delay, LANES), :]
    halo_out[0:LANES, :] = (q[begin:, :].astype(F32) * total).astype(BF16)
    last = kv[LANES + 8:, :]
    high = last.astype(BF16).astype(F32)
    halo_out[LANES:LANES + 16, :] = jnp.concatenate([high, last - high], axis=0).astype(BF16)


def edge(q, k, v, params):
    rows, chans = q.shape
    wide = math.gcd(chans, 512)
    tall = math.gcd(rows, 256)
    last = pl.BlockSpec((tall, wide), lambda i: (rows // tall - 1, i))
    column = lambda height: pl.BlockSpec((height, wide), lambda i: (0, i))
    return pl.pallas_call(
        edge_kernel,
        grid=(chans // wide,),
        out_shape=jax.ShapeDtypeStruct((LANES + 16, chans), BF16),
        in_specs=[last] * 3 + [column(params.shape[0])],
        out_specs=column(LANES + 16),
        scratch_shapes=[pltpu.VMEM((LANES + 16, wide), F32)],
        compiler_params=pltpu.CompilerParams(vmem_limit_bytes=MIX_VMEM),
        name="edge",
    )(q, k, v, params)


def mix_kernel(q, k, v, halo, params, late_params, medium_taps, y_out, state_out, gated, y_t, seconds,
               first_a, key_a, first_b, key_b):
    parity = pl.program_id(0) % 2

    @pl.when(parity == 0)
    def _():
        mix_strip(q, k, v, halo, params, late_params, medium_taps, y_out, state_out, gated, y_t, seconds,
                  (first_a, key_a), (first_b, key_b))

    @pl.when(parity == 1)
    def _():
        mix_strip(q, k, v, halo, params, late_params, medium_taps, y_out, state_out, gated, y_t, seconds,
                  (first_b, key_b), (first_a, key_a))


def mix_strip(q, k, v, halo, params, late_params, medium_taps, y_out, state_out, gated, y_t, seconds,
              fresh_refs, ready_refs):
    rows = q.shape[0]
    blocks = rows // WIDE
    halves = rows // LANES
    next_first, next_key = fresh_refs
    first_t, key_t = ready_refs
    row_i = lax.broadcasted_iota(jnp.int32, (LANES, LANES), 0)
    col_i = lax.broadcasted_iota(jnp.int32, (LANES, LANES), 1)
    causal = col_i >= row_i
    zero = jnp.zeros((LANES, LANES), BF16)
    time_down = lax.broadcasted_iota(jnp.int32, (WIDE, LANES), 0).astype(F32)
    time_along = lax.broadcasted_iota(jnp.int32, (LANES, WIDE), 1).astype(F32)
    lane_group = lax.broadcasted_iota(jnp.int32, (WIDE, LANES), 1) // MODES
    taps = params[...]
    late = late_params[...]

    def gate_first(b):
        begin = b * LANES
        part = pl.ds(begin, LANES)
        keys = k[part, :]
        fresh = keys.astype(F32) * v[part, :].astype(F32)
        gated[pl.ds(begin + 8, LANES), :] = fresh
        total = taps[0:1, :] * fresh
        for delay in range(1, SHORT):
            total = total + taps[delay:delay + 1, :] * gated[pl.ds(begin + 8 - delay, LANES), :]
        first = (q[part, :].astype(F32) * total).astype(BF16)
        next_first[:, begin + LANES:begin + 2 * LANES] = first.T
        next_key[:, begin:begin + LANES] = keys.T

    def medium_of(g):
        chans = pl.ds(g * GROUP_CH, GROUP_CH)
        turned = jnp.broadcast_to(medium_taps[g:g + 1, :], (LANES, LANES))
        turned = pltpu.roll(turned, 0, 1, stride=1, stride_axis=0)
        medium_w = jnp.concatenate(
            [jnp.where(causal, 0.0, turned), jnp.where(causal, turned, 0.0)], axis=0).astype(BF16)
        window = jnp.concatenate([first_t[chans, b * LANES:(b + 2) * LANES] for b in range(halves)], axis=0)
        medium = jnp.dot(window, medium_w, preferred_element_type=F32)
        key = jnp.concatenate([key_t[chans, b * LANES:(b + 1) * LANES] for b in range(halves)], axis=0)
        second = (key.astype(F32) * medium).astype(BF16)
        for b in range(halves):
            seconds[(b // 2) * GROUP_CH:(b // 2 + 1) * GROUP_CH,
                    g * WIDE + (b % 2) * LANES:g * WIDE + (b % 2 + 1) * LANES] = (
                second[b * GROUP_CH:(b + 1) * GROUP_CH])

    gated[0:8, :] = halo[LANES:LANES + 8, :].astype(F32) + halo[LANES + 8:LANES + 16, :].astype(F32)
    next_first[:, 0:LANES] = halo[0:LANES, :].T
    early = EARLY * halves // 16
    done = 0
    for g in range(PACK):
        medium_of(g)
        goal = early * (g + 1) // PACK
        for b in range(done, goal):
            gate_first(b)
        done = goal

    rate = late[RATE:RATE + 1, :]
    tails = jnp.exp(-rate * (WIDE - 1.0 - time_down)).astype(BF16)
    tails_w = jnp.concatenate([jnp.where(lane_group == g, tails, jnp.zeros_like(tails)) for g in range(PACK)], axis=0)
    sums = jnp.dot(seconds[...], tails_w, preferred_element_type=F32)
    decay = jnp.exp(-rate * float(WIDE))
    state = jnp.zeros((GROUP_CH, LANES), F32)
    states = []
    for b in range(blocks):
        states.append(state)
        state = decay * state + sums[b * GROUP_CH:(b + 1) * GROUP_CH, :]
    state_out[...] = state.astype(BF16)
    carried = jnp.concatenate(split2(jnp.concatenate(states, axis=0)), axis=1)

    down = lambda row: jnp.broadcast_to(late[row:row + 1, :], (LANES, LANES)).T
    rate_t, amp_t, skip_t = down(RATE), down(AMP), down(SKIP)
    both = lambda half: jnp.concatenate([half, half], axis=1)
    power = both(amp_t) * jnp.exp(-both(rate_t) * time_along)
    lead = (power * jnp.exp(-both(rate_t))).astype(BF16)

    def long_of(g):
        chans = pl.ds(g * GROUP_CH, GROUP_CH)
        mine = slice(g * MODES, (g + 1) * MODES)
        profile = jnp.sum(power[mine], axis=0, keepdims=True)
        turned = pltpu.roll(jnp.broadcast_to(profile, (LANES, WIDE)), 0, 1, stride=1, stride_axis=0)
        near = jnp.where(causal, turned[:, :LANES], 0.0).astype(BF16)
        pieces = [jnp.concatenate([near, turned[:, LANES:].astype(BF16)], axis=1),
                  jnp.concatenate([zero, near], axis=1)]
        lead_g = [lead[mine]]
        if g > 0:
            lead_g = [jnp.zeros((g * MODES, WIDE), BF16)] + lead_g
        if g < PACK - 1:
            lead_g = lead_g + [jnp.zeros(((PACK - 1 - g) * MODES, WIDE), BF16)]
        second = seconds[:, g * WIDE:(g + 1) * WIDE]
        y = jnp.dot(jnp.concatenate([second, carried], axis=1),
                    jnp.concatenate(pieces + lead_g + lead_g, axis=0), preferred_element_type=F32)
        gain = both(skip_t[g * GROUP_CH:(g + 1) * GROUP_CH, :])
        gain = jnp.concatenate([gain] * blocks, axis=0)
        y = (y + gain * second.astype(F32)).astype(BF16)
        for b in range(blocks):
            y_t[chans, b * WIDE:(b + 1) * WIDE] = y[b * GROUP_CH:(b + 1) * GROUP_CH, :]

    for g in range(PACK):
        long_of(g)
        goal = early + (halves - early) * (g + 1) // PACK
        for b in range(done, goal):
            gate_first(b)
        done = goal
    for begin in range(0, rows, LANES):
        y_out[pl.ds(begin, LANES), :] = y_t[:, begin:begin + LANES].T


def mix(q, k, v, halo, params, medium_taps):
    rows, chans = q.shape
    strips = chans // LANES
    ahead = lambda i: jnp.minimum(i, strips - 1)
    behind = lambda i: jnp.maximum(i - 1, 0)
    column = lambda height, of: pl.BlockSpec((height, LANES), lambda i: (0, of(i)))
    return pl.pallas_call(
        mix_kernel,
        grid=(strips + 1,),
        out_shape=(jax.ShapeDtypeStruct((rows, chans), BF16), jax.ShapeDtypeStruct((GROUP_CH, chans), BF16)),
        in_specs=[column(rows, ahead)] * 3 + [
            column(halo.shape[0], ahead), column(params.shape[0], ahead), column(params.shape[0], behind),
            pl.BlockSpec((PACK, LANES), lambda i: (behind(i), 0))],
        out_specs=(column(rows, behind), column(GROUP_CH, behind)),
        scratch_shapes=[
            pltpu.VMEM((rows + 8, LANES), F32),
            pltpu.VMEM((LANES, rows), BF16),
            pltpu.VMEM((LANES, PACK * WIDE), BF16),
        ] + [pltpu.VMEM((LANES, rows + LANES), BF16), pltpu.VMEM((LANES, rows), BF16)] * 2,
        compiler_params=pltpu.CompilerParams(vmem_limit_bytes=MIX_VMEM),
        cost_estimate=pl.CostEstimate(flops=8 * rows * chans * WIDE, bytes_accessed=8 * rows * chans, transcendentals=0),
        name="mix",
    )(q, k, v, halo, params, params, medium_taps)


def join_kernel(y, v, states, weights, params, mixed_out, energy_out, energy):
    rows, wide = y.shape
    step = pl.program_id(0)

    @pl.when(step == 0)
    def _():
        energy[...] = jnp.zeros_like(energy)

    row_i = lax.broadcasted_iota(jnp.int32, (LANES, LANES), 0)
    col_i = lax.broadcasted_iota(jnp.int32, (LANES, LANES), 1)
    own = row_i // GROUP_CH == col_i // MODES
    time = row_i.astype(F32) + 1.0
    entry = jnp.zeros((GROUP_CH, wide), F32)
    for source in range(states.shape[0]):
        entry = entry + weights[source:source + 1, :] * states[source].astype(F32)
    entries, leads = [], []
    for s in range(wide // LANES):
        here = slice(s * LANES, (s + 1) * LANES)
        spread = jnp.where(own, jnp.concatenate([entry[:, here]] * PACK, axis=0), 0.0)
        entries.append(jnp.concatenate(split2(spread), axis=1))
        leads.append(jnp.exp(-params[RATE:RATE + 1, here] * time))
    for b in range(rows // LANES):
        part = pl.ds(b * LANES, LANES)
        total = energy[part, :]
        for s in range(wide // LANES):
            here = slice(s * LANES, (s + 1) * LANES)
            lead = (leads[s] * jnp.exp(-params[RATE:RATE + 1, here] * float(b * LANES))).astype(BF16)
            carried = lax.dot_general(jnp.concatenate([lead, lead], axis=1), entries[s],
                                      (((1,), (1,)), ((), ())), preferred_element_type=F32)
            mixed = v[part, here].astype(F32) * (y[part, here].astype(F32) + carried)
            mixed_out[part, here] = mixed.astype(BF16)
            total = total + mixed * mixed
        energy[part, :] = total

    @pl.when(step == pl.num_programs(0) - 1)
    def _():
        for begin in range(0, rows, LANES):
            energy_out[:, begin:begin + LANES] = jnp.sum(energy[pl.ds(begin, LANES), :].T, axis=0, keepdims=True)


def join(y, v, states, weights, params):
    rows, chans = y.shape
    wide = math.gcd(chans, JOIN_STRIP)
    column = lambda height: pl.BlockSpec((height, wide), lambda i: (0, i))
    return pl.pallas_call(
        join_kernel,
        grid=(chans // wide,),
        out_shape=(jax.ShapeDtypeStruct((rows, chans), BF16), jax.ShapeDtypeStruct((1, rows), F32)),
        in_specs=[column(rows), column(rows), pl.BlockSpec((states.shape[0], GROUP_CH, wide), lambda i: (0, 0, i)),
                  column(weights.shape[0]), column(params.shape[0])],
        out_specs=(column(rows), pl.BlockSpec((1, rows), lambda i: (0, 0))),
        scratch_shapes=[pltpu.VMEM((rows, LANES), F32)],
        compiler_params=pltpu.CompilerParams(vmem_limit_bytes=JOIN_VMEM),
        cost_estimate=pl.CostEstimate(flops=2 * rows * chans * WIDE, bytes_accessed=6 * rows * chans, transcendentals=0),
        name="join",
    )(y, v, states, weights, params)


def scale_kernel(mixed, energy, gain, out, *, width):
    rows, chans = mixed.shape
    for begin in range(0, rows, LANES):
        part = pl.ds(begin, LANES)
        scale = lax.rsqrt(energy[:, begin:begin + LANES] / width + 1e-06)
        scale = jnp.broadcast_to(scale, (LANES, LANES)).T
        for left in range(0, chans, LANES):
            here = slice(left, left + LANES)
            out[part, here] = (mixed[part, here].astype(F32) * scale * gain[:, here]).astype(BF16)


def scaled(mixed, energy, gain, width):
    rows, chans = mixed.shape
    tall = math.gcd(rows, 256)
    block = pl.BlockSpec((tall, chans), lambda i: (i, 0))
    return pl.pallas_call(
        functools.partial(scale_kernel, width=width),
        grid=(rows // tall,),
        out_shape=jax.ShapeDtypeStruct((rows, chans), BF16),
        in_specs=[block, pl.BlockSpec((1, tall), lambda i: (0, i)), pl.BlockSpec((1, chans), lambda i: (0, 0))],
        out_specs=block,
        compiler_params=pltpu.CompilerParams(vmem_limit_bytes=JOIN_VMEM),
        name="scale",
    )(mixed, energy, gain)


def local(queries, key_rows, value_rows, short_filter, medium_filter, decays, residue, skip_gain,
          norm_gain, width):
    rows, chans = queries.shape
    amplitude = residue * jnp.sqrt(-jnp.expm1(-2.0 * decays))
    params = jnp.concatenate([
        jnp.repeat(short_filter, GROUP_CH, axis=1),
        decays.reshape(1, chans), amplitude.reshape(1, chans), skip_gain[None, :],
        jnp.zeros((16 - SHORT - 3, chans), F32)], axis=0)
    halo = passed_along(edge(queries, key_rows, value_rows, params), "context", 1)
    y, state = mix(queries, key_rows, value_rows, halo, params, medium_filter.T.astype(F32))
    states = lax.all_gather(state, "context")
    count = lax.axis_size("context")
    gap = (lax.axis_index("context") - 1 - jnp.arange(count)).astype(F32)[:, None]
    weights = jnp.where(gap >= 0.0, params[AMP:AMP + 1] * jnp.exp(-params[RATE:RATE + 1] * (jnp.maximum(gap, 0.0) * rows)), 0.0)
    mixed, energy = join(y, value_rows, states, weights, params)
    energy = lax.psum(energy, "tensor")
    return scaled(mixed, energy, norm_gain[None, :], width)


def solution(mesh):
    def whole(*args):
        return jax.shard_map(
            functools.partial(local, width=args[0].shape[1]),
            mesh=mesh,
            in_specs=(
                P("context", "tensor"),
                P("context", "tensor"),
                P("context", "tensor"),
                P(None, "tensor"),
                P(None, "tensor"),
                P("tensor", None),
                P("tensor", None),
                P("tensor"),
                P("tensor"),
            ),
            out_specs=P("context", "tensor"),
            check_vma=False,
        )(*args)

    return whole
```

```python
import functools
import math

import jax
import jax.numpy as jnp
from jax import lax
from jax.experimental import pallas as pl
from jax.experimental.pallas import tpu as pltpu
from jax.sharding import PartitionSpec as P

GROUP_CH = 16
LANES = 128
PACK = LANES // GROUP_CH
WIDE = 256
MODES = 16
SHORT = 7
RATE, AMP, SKIP = SHORT, SHORT + 1, SHORT + 2
EARLY = 0
EDGE_PARTS = 1
JOIN_STRIP = 512
TALL = 256
MIX_VMEM = 24 << 20
JOIN_VMEM = 24 << 20
F32 = jnp.float32
BF16 = jnp.bfloat16


def split2(value):
    high = value.astype(BF16)
    return high, (value - high.astype(F32)).astype(BF16)


def passed_along(value, axis, steps):
    count = lax.axis_size(axis)
    return lax.ppermute(value, axis, [(source, source + steps) for source in range(count - steps)])


def edge_kernel(q, k, v, short_filter, halo_out, gated):
    rows, wide = q.shape
    begin = rows - LANES
    pack = wide // GROUP_CH
    spread = (lax.broadcasted_iota(jnp.int32, (pack, wide), 1) // GROUP_CH
              == lax.broadcasted_iota(jnp.int32, (pack, wide), 0)).astype(F32)
    taps = jnp.dot(short_filter[...], spread, precision=lax.Precision.HIGHEST, preferred_element_type=F32)
    kv = k[begin - 16:, :].astype(F32) * v[begin - 16:, :].astype(F32)
    gated[...] = kv
    total = taps[0:1, :] * gated[16:, :]
    for delay in range(1, SHORT):
        total = total + taps[delay:delay + 1, :] * gated[pl.ds(16 - delay, LANES), :]
    halo_out[0:LANES, :] = (q[begin:, :].astype(F32) * total).astype(BF16)
    last = kv[LANES + 8:, :]
    high = last.astype(BF16).astype(F32)
    halo_out[LANES:LANES + 16, :] = jnp.concatenate([high, last - high], axis=0).astype(BF16)


def edge(q, k, v, short_filter):
    rows, chans = q.shape
    wide = chans // EDGE_PARTS
    tall = math.gcd(rows, 256)
    last = pl.BlockSpec((tall, wide), lambda i: (rows // tall - 1, i))
    column = lambda height, width: pl.BlockSpec((height, width), lambda i: (0, i))
    if wide // GROUP_CH % LANES:
        short_filter = short_filter.reshape(SHORT, EDGE_PARTS, wide // GROUP_CH).transpose(1, 0, 2)
        tap_spec = pl.BlockSpec((pl.Squeezed(), SHORT, wide // GROUP_CH), lambda i: (i, 0, 0))
    else:
        tap_spec = column(SHORT, wide // GROUP_CH)
    return pl.pallas_call(
        edge_kernel,
        grid=(EDGE_PARTS,),
        out_shape=jax.ShapeDtypeStruct((LANES + 16, chans), BF16),
        in_specs=[last] * 3 + [tap_spec],
        out_specs=column(LANES + 16, wide),
        scratch_shapes=[pltpu.VMEM((LANES + 16, wide), F32)],
        compiler_params=pltpu.CompilerParams(vmem_limit_bytes=MIX_VMEM),
        name="edge",
    )(q, k, v, short_filter)


def mix_kernel(q, k, v, halo, params, late_params, medium_taps, y_out, state_out, gated, y_t, seconds,
               first_a, key_a, first_b, key_b):
    parity = pl.program_id(0) % 2

    @pl.when(parity == 0)
    def _():
        mix_strip(q, k, v, halo, params, late_params, medium_taps, y_out, state_out, gated, y_t, seconds,
                  (first_a, key_a), (first_b, key_b))

    @pl.when(parity == 1)
    def _():
        mix_strip(q, k, v, halo, params, late_params, medium_taps, y_out, state_out, gated, y_t, seconds,
                  (first_b, key_b), (first_a, key_a))


def mix_strip(q, k, v, halo, params, late_params, medium_taps, y_out, state_out, gated, y_t, seconds,
              fresh_refs, ready_refs):
    rows = q.shape[0]
    blocks = rows // WIDE
    halves = rows // LANES
    next_first, next_key = fresh_refs
    first_t, key_t = ready_refs
    row_i = lax.broadcasted_iota(jnp.int32, (LANES, LANES), 0)
    col_i = lax.broadcasted_iota(jnp.int32, (LANES, LANES), 1)
    causal = col_i >= row_i
    zero = jnp.zeros((LANES, LANES), BF16)
    time_down = lax.broadcasted_iota(jnp.int32, (WIDE, LANES), 0).astype(F32)
    time_along = lax.broadcasted_iota(jnp.int32, (LANES, WIDE), 1).astype(F32)
    lane_group = lax.broadcasted_iota(jnp.int32, (WIDE, LANES), 1) // MODES
    taps = params[...]
    late = late_params[...]

    def gate_first(b):
        begin = b * LANES
        part = pl.ds(begin, LANES)
        keys = k[part, :]
        fresh = keys.astype(F32) * v[part, :].astype(F32)
        gated[pl.ds(begin + 8, LANES), :] = fresh
        total = taps[0:1, :] * fresh
        for delay in range(1, SHORT):
            total = total + taps[delay:delay + 1, :] * gated[pl.ds(begin + 8 - delay, LANES), :]
        first = (q[part, :].astype(F32) * total).astype(BF16)
        next_first[:, begin + LANES:begin + 2 * LANES] = first.T
        next_key[:, begin:begin + LANES] = keys.T

    def medium_of(g):
        chans = pl.ds(g * GROUP_CH, GROUP_CH)
        turned = jnp.broadcast_to(medium_taps[g:g + 1, :], (LANES, LANES))
        turned = pltpu.roll(turned, 0, 1, stride=1, stride_axis=0)
        medium_w = jnp.concatenate(
            [jnp.where(causal, 0.0, turned), jnp.where(causal, turned, 0.0)], axis=0).astype(BF16)
        window = jnp.concatenate([first_t[chans, b * LANES:(b + 2) * LANES] for b in range(halves)], axis=0)
        medium = jnp.dot(window, medium_w, preferred_element_type=F32)
        key = jnp.concatenate([key_t[chans, b * LANES:(b + 1) * LANES] for b in range(halves)], axis=0)
        second = (key.astype(F32) * medium).astype(BF16)
        for b in range(halves):
            seconds[(b // 2) * GROUP_CH:(b // 2 + 1) * GROUP_CH,
                    g * WIDE + (b % 2) * LANES:g * WIDE + (b % 2 + 1) * LANES] = (
                second[b * GROUP_CH:(b + 1) * GROUP_CH])

    gated[0:8, :] = halo[LANES:LANES + 8, :].astype(F32) + halo[LANES + 8:LANES + 16, :].astype(F32)
    next_first[:, 0:LANES] = halo[0:LANES, :].T
    early = EARLY * halves // 16
    done = 0
    for g in range(PACK):
        medium_of(g)
        goal = early * (g + 1) // PACK
        for b in range(done, goal):
            gate_first(b)
        done = goal

    rate = late[RATE:RATE + 1, :]
    tails = jnp.exp(-rate * (WIDE - 1.0 - time_down)).astype(BF16)
    tails_w = jnp.concatenate([jnp.where(lane_group == g, tails, jnp.zeros_like(tails)) for g in range(PACK)], axis=0)
    sums = jnp.dot(seconds[...], tails_w, preferred_element_type=F32)
    decay = jnp.exp(-rate * float(WIDE))
    state = jnp.zeros((GROUP_CH, LANES), F32)
    states = []
    for b in range(blocks):
        states.append(state)
        state = decay * state + sums[b * GROUP_CH:(b + 1) * GROUP_CH, :]
    state_out[...] = state.astype(BF16)
    carried = jnp.concatenate(split2(jnp.concatenate(states, axis=0)), axis=1)

    down = lambda row: jnp.broadcast_to(late[row:row + 1, :], (LANES, LANES)).T
    rate_t, amp_t, skip_t = down(RATE), down(AMP), down(SKIP)
    both = lambda half: jnp.concatenate([half, half], axis=1)
    power = both(amp_t) * jnp.exp(-both(rate_t) * time_along)
    lead = (power * jnp.exp(-both(rate_t))).astype(BF16)

    def long_of(g):
        chans = pl.ds(g * GROUP_CH, GROUP_CH)
        mine = slice(g * MODES, (g + 1) * MODES)
        profile = jnp.sum(power[mine], axis=0, keepdims=True)
        turned = pltpu.roll(jnp.broadcast_to(profile, (LANES, WIDE)), 0, 1, stride=1, stride_axis=0)
        near = jnp.where(causal, turned[:, :LANES], 0.0).astype(BF16)
        pieces = [jnp.concatenate([near, turned[:, LANES:].astype(BF16)], axis=1),
                  jnp.concatenate([zero, near], axis=1)]
        lead_g = [lead[mine]]
        if g > 0:
            lead_g = [jnp.zeros((g * MODES, WIDE), BF16)] + lead_g
        if g < PACK - 1:
            lead_g = lead_g + [jnp.zeros(((PACK - 1 - g) * MODES, WIDE), BF16)]
        second = seconds[:, g * WIDE:(g + 1) * WIDE]
        y = jnp.dot(jnp.concatenate([second, carried], axis=1),
                    jnp.concatenate(pieces + lead_g + lead_g, axis=0), preferred_element_type=F32)
        gain = both(skip_t[g * GROUP_CH:(g + 1) * GROUP_CH, :])
        gain = jnp.concatenate([gain] * blocks, axis=0)
        y = (y + gain * second.astype(F32)).astype(BF16)
        for b in range(blocks):
            y_t[chans, b * WIDE:(b + 1) * WIDE] = y[b * GROUP_CH:(b + 1) * GROUP_CH, :]

    for g in range(PACK):
        long_of(g)
        goal = early + (halves - early) * (g + 1) // PACK
        for b in range(done, goal):
            gate_first(b)
        done = goal
    for begin in range(0, rows, LANES):
        y_out[pl.ds(begin, LANES), :] = y_t[:, begin:begin + LANES].T


def mix(q, k, v, halo, params, medium_taps):
    rows, chans = q.shape
    strips = chans // LANES
    ahead = lambda i: jnp.minimum(i, strips - 1)
    behind = lambda i: jnp.maximum(i - 1, 0)
    column = lambda height, of: pl.BlockSpec((height, LANES), lambda i: (0, of(i)))
    return pl.pallas_call(
        mix_kernel,
        grid=(strips + 1,),
        out_shape=(jax.ShapeDtypeStruct((rows, chans), BF16), jax.ShapeDtypeStruct((GROUP_CH, chans), BF16)),
        in_specs=[column(rows, ahead)] * 3 + [
            column(halo.shape[0], ahead), column(params.shape[0], ahead), column(params.shape[0], behind),
            pl.BlockSpec((PACK, LANES), lambda i: (behind(i), 0))],
        out_specs=(column(rows, behind), column(GROUP_CH, behind)),
        scratch_shapes=[
            pltpu.VMEM((rows + 8, LANES), F32),
            pltpu.VMEM((LANES, rows), BF16),
            pltpu.VMEM((LANES, PACK * WIDE), BF16),
        ] + [pltpu.VMEM((LANES, rows + LANES), BF16), pltpu.VMEM((LANES, rows), BF16)] * 2,
        compiler_params=pltpu.CompilerParams(vmem_limit_bytes=MIX_VMEM),
        cost_estimate=pl.CostEstimate(flops=8 * rows * chans * WIDE, bytes_accessed=8 * rows * chans, transcendentals=0),
        name="mix",
    )(q, k, v, halo, params, params, medium_taps)


def join_kernel(y, v, states, weights, params, mixed_out, energy_out, energy):
    rows, wide = y.shape
    step = pl.program_id(0)

    @pl.when(step == 0)
    def _():
        energy[...] = jnp.zeros_like(energy)

    own = (lax.broadcasted_iota(jnp.int32, (WIDE, WIDE), 0) // GROUP_CH
           == lax.broadcasted_iota(jnp.int32, (WIDE, WIDE), 1) // MODES)
    time = lax.broadcasted_iota(jnp.int32, (TALL, WIDE), 0).astype(F32) + 1.0
    entry = jnp.zeros((GROUP_CH, wide), F32)
    for source in range(states.shape[0]):
        entry = entry + weights[source:source + 1, :] * states[source].astype(F32)
    for s in range(wide // WIDE):
        here = slice(s * WIDE, (s + 1) * WIDE)
        rate = params[RATE:RATE + 1, here]
        spread = jnp.concatenate([entry[:, here]] * (WIDE // GROUP_CH), axis=0)
        spread = jnp.where(own, spread, 0.0).astype(BF16)
        lead = jnp.exp(-rate * time)
        for b in range(rows // TALL):
            part = pl.ds(b * TALL, TALL)
            faded = (lead * jnp.exp(-rate * float(b * TALL))).astype(BF16)
            carried = lax.dot_general(faded, spread, (((1,), (1,)), ((), ())), preferred_element_type=F32)
            mixed = v[part, here].astype(F32) * (y[part, here].astype(F32) + carried)
            mixed_out[part, here] = mixed.astype(BF16)
            square = mixed * mixed
            energy[part, :] += square[:, :LANES] + square[:, LANES:]

    @pl.when(step == pl.num_programs(0) - 1)
    def _():
        for begin in range(0, rows, LANES):
            energy_out[:, begin:begin + LANES] = jnp.sum(energy[pl.ds(begin, LANES), :].T, axis=0, keepdims=True)


def join(y, v, states, weights, params):
    rows, chans = y.shape
    wide = math.gcd(chans, JOIN_STRIP)
    column = lambda height: pl.BlockSpec((height, wide), lambda i: (0, i))
    return pl.pallas_call(
        join_kernel,
        grid=(chans // wide,),
        out_shape=(jax.ShapeDtypeStruct((rows, chans), BF16), jax.ShapeDtypeStruct((1, rows), F32)),
        in_specs=[column(rows), column(rows), pl.BlockSpec((states.shape[0], GROUP_CH, wide), lambda i: (0, 0, i)),
                  column(weights.shape[0]), column(params.shape[0])],
        out_specs=(column(rows), pl.BlockSpec((1, rows), lambda i: (0, 0))),
        scratch_shapes=[pltpu.VMEM((rows, LANES), F32)],
        compiler_params=pltpu.CompilerParams(vmem_limit_bytes=JOIN_VMEM),
        cost_estimate=pl.CostEstimate(flops=2 * rows * chans * WIDE, bytes_accessed=6 * rows * chans, transcendentals=0),
        name="join",
    )(y, v, states, weights, params)


def scale_kernel(mixed, energy, gain, out, *, width):
    rows, chans = mixed.shape
    for begin in range(0, rows, LANES):
        part = pl.ds(begin, LANES)
        scale = jnp.sum(energy[:, begin:begin + LANES], axis=0, keepdims=True)
        scale = lax.rsqrt(scale / width + 1e-06)
        scale = jnp.broadcast_to(scale, (LANES, LANES)).T
        for left in range(0, chans, LANES):
            here = slice(left, left + LANES)
            out[part, here] = (mixed[part, here].astype(F32) * scale * gain[:, here]).astype(BF16)


def scaled(mixed, energy, gain, width):
    rows, chans = mixed.shape
    tall = math.gcd(rows, 512)
    block = pl.BlockSpec((tall, chans), lambda i: (i, 0))
    return pl.pallas_call(
        functools.partial(scale_kernel, width=width),
        grid=(rows // tall,),
        out_shape=jax.ShapeDtypeStruct((rows, chans), BF16),
        in_specs=[block, pl.BlockSpec((energy.shape[0], tall), lambda i: (0, i)), pl.BlockSpec((1, chans), lambda i: (0, 0))],
        out_specs=block,
        compiler_params=pltpu.CompilerParams(vmem_limit_bytes=JOIN_VMEM),
        name="scale",
    )(mixed, energy, gain)


def local(queries, key_rows, value_rows, short_filter, medium_filter, decays, residue, skip_gain,
          norm_gain, width):
    rows, chans = queries.shape
    queries, key_rows, value_rows = (pltpu.with_memory_space_constraint(array, pltpu.HBM)
                                     for array in (queries, key_rows, value_rows))
    amplitude = residue * jnp.sqrt(-jnp.expm1(-2.0 * decays))
    params = jnp.concatenate([
        jnp.repeat(short_filter, GROUP_CH, axis=1),
        decays.reshape(1, chans), amplitude.reshape(1, chans), skip_gain[None, :],
        jnp.zeros((16 - SHORT - 3, chans), F32)], axis=0)
    halo = passed_along(edge(queries, key_rows, value_rows, short_filter), "context", 1)
    y, state = mix(queries, key_rows, value_rows, halo, params, medium_filter.T.astype(F32))
    states = lax.all_gather(state, "context")
    count = lax.axis_size("context")
    gap = (lax.axis_index("context") - 1 - jnp.arange(count)).astype(F32)[:, None]
    weights = jnp.where(gap >= 0.0, params[AMP:AMP + 1] * jnp.exp(-params[RATE:RATE + 1] * (jnp.maximum(gap, 0.0) * rows)), 0.0)
    y = pltpu.with_memory_space_constraint(y, pltpu.VMEM)
    mixed, energy = join(y, value_rows, states, weights, params)
    energy = lax.all_gather(energy, "tensor", tiled=True)
    mixed = pltpu.with_memory_space_constraint(mixed, pltpu.VMEM)
    return scaled(mixed, energy, norm_gain[None, :], width)


def solution(mesh):
    def whole(*args):
        return jax.shard_map(
            functools.partial(local, width=args[0].shape[1]),
            mesh=mesh,
            in_specs=(
                P("context", "tensor"),
                P("context", "tensor"),
                P("context", "tensor"),
                P(None, "tensor"),
                P(None, "tensor"),
                P("tensor", None),
                P("tensor", None),
                P("tensor"),
                P("tensor"),
            ),
            out_specs=P("context", "tensor"),
            check_vma=False,
        )(*args)

    return whole
```

```python
import functools
import math

import jax
import jax.numpy as jnp
from jax import lax
from jax.experimental import pallas as pl
from jax.experimental.pallas import tpu as pltpu
from jax.sharding import PartitionSpec as P

GROUP_CH = 16
LANES = 128
PACK = LANES // GROUP_CH
WIDE = 256
MODES = 16
SHORT = 7
RATE, AMP, SKIP = SHORT, SHORT + 1, SHORT + 2
GATE_STRIP = 256
MIX_STRIP = 256
EDGE_PARTS = 1
JOIN_STRIP = 512
MIX_VMEM = 24 << 20
JOIN_VMEM = 24 << 20
F32 = jnp.float32
BF16 = jnp.bfloat16


def split2(value):
    high = value.astype(BF16)
    return high, (value - high.astype(F32)).astype(BF16)


def passed_along(value, axis, steps):
    count = lax.axis_size(axis)
    return lax.ppermute(value, axis, [(source, source + steps) for source in range(count - steps)])


def edge_kernel(q, k, v, short_filter, halo_out, gated):
    rows, wide = q.shape
    begin = rows - LANES
    pack = wide // GROUP_CH
    spread = (lax.broadcasted_iota(jnp.int32, (pack, wide), 1) // GROUP_CH
              == lax.broadcasted_iota(jnp.int32, (pack, wide), 0)).astype(F32)
    taps = jnp.dot(short_filter[...], spread, precision=lax.Precision.HIGHEST, preferred_element_type=F32)
    kv = k[begin - 16:, :].astype(F32) * v[begin - 16:, :].astype(F32)
    gated[...] = kv
    total = taps[0:1, :] * gated[16:, :]
    for delay in range(1, SHORT):
        total = total + taps[delay:delay + 1, :] * gated[pl.ds(16 - delay, LANES), :]
    halo_out[0:LANES, :] = (q[begin:, :].astype(F32) * total).astype(BF16)
    last = kv[LANES + 8:, :]
    high = last.astype(BF16).astype(F32)
    halo_out[LANES:LANES + 16, :] = jnp.concatenate([high, last - high], axis=0).astype(BF16)


def edge(q, k, v, short_filter):
    rows, chans = q.shape
    wide = chans // EDGE_PARTS
    tall = math.gcd(rows, 256)
    last = pl.BlockSpec((tall, wide), lambda i: (rows // tall - 1, i))
    column = lambda height, width: pl.BlockSpec((height, width), lambda i: (0, i))
    if wide // GROUP_CH % LANES:
        short_filter = short_filter.reshape(SHORT, EDGE_PARTS, wide // GROUP_CH).transpose(1, 0, 2)
        tap_spec = pl.BlockSpec((pl.Squeezed(), SHORT, wide // GROUP_CH), lambda i: (i, 0, 0))
    else:
        tap_spec = column(SHORT, wide // GROUP_CH)
    return pl.pallas_call(
        edge_kernel,
        grid=(EDGE_PARTS,),
        out_shape=jax.ShapeDtypeStruct((LANES + 16, chans), BF16),
        in_specs=[last] * 3 + [tap_spec],
        out_specs=column(LANES + 16, wide),
        scratch_shapes=[pltpu.VMEM((LANES + 16, wide), F32)],
        compiler_params=pltpu.CompilerParams(vmem_limit_bytes=MIX_VMEM),
        name="edge",
    )(q, k, v, short_filter)


def gate_kernel(q, k, v, params, first_out, key_out, *gated_refs):
    rows, wide = q.shape
    for s, gated in enumerate(gated_refs):
        here = slice(s * LANES, (s + 1) * LANES)
        taps = params[:, here]
        gated[0:8, :] = jnp.zeros((8, LANES), F32)
        for begin in range(0, rows, LANES):
            part = pl.ds(begin, LANES)
            keys = k[part, here]
            fresh = keys.astype(F32) * v[part, here].astype(F32)
            gated[pl.ds(begin + 8, LANES), :] = fresh
            total = taps[0:1, :] * fresh
            for delay in range(1, SHORT):
                total = total + taps[delay:delay + 1, :] * gated[pl.ds(begin + 8 - delay, LANES), :]
            first = (q[part, here].astype(F32) * total).astype(BF16)
            first_out[here, begin:begin + LANES] = first.T
            key_out[here, begin:begin + LANES] = keys.T


def gate(q, k, v, params):
    rows, chans = q.shape
    column = lambda height: pl.BlockSpec((height, GATE_STRIP), lambda i: (0, i))
    down = pl.BlockSpec((GATE_STRIP, rows), lambda i: (i, 0))
    return pl.pallas_call(
        gate_kernel,
        grid=(chans // GATE_STRIP,),
        out_shape=(jax.ShapeDtypeStruct((chans, rows), BF16),) * 2,
        in_specs=[column(rows)] * 3 + [column(params.shape[0])],
        out_specs=(down, down),
        scratch_shapes=[pltpu.VMEM((rows + 8, LANES), F32)] * (GATE_STRIP // LANES),
        compiler_params=pltpu.CompilerParams(vmem_limit_bytes=MIX_VMEM),
        cost_estimate=pl.CostEstimate(flops=64 * rows * chans, bytes_accessed=10 * rows * chans, transcendentals=0),
        name="gate",
    )(q, k, v, params)


def summed(value, axis):
    count = lax.axis_size(axis)
    if count & (count - 1):
        return lax.psum(value, axis)
    step = 1
    while step < count:
        value = value + lax.ppermute(value, axis, [(source, source ^ step) for source in range(count)])
        step *= 2
    return value


def mix_kernel(first, keys_t, halo, q, k, v, params, medium_taps, y_out, carry_out, state_out, *scratch):
    strips = first.shape[0] // LANES
    for s in range(strips):
        here = slice(s * LANES, (s + 1) * LANES)
        mix_strip(first.at[here, :], keys_t.at[here, :], halo.at[:, here], q.at[:, here], k.at[:, here], v.at[:, here],
                  params.at[:, here], medium_taps.at[s * PACK:(s + 1) * PACK, :],
                  y_out.at[:, here], carry_out.at[:, here], state_out.at[:, here], *scratch[4 * s:4 * s + 4])


def mix_strip(first_t, key_t, halo, q, k, v, late_params, medium_taps, y_out, carry_out, state_out, y_t, seconds,
              gated, start):
    rows = first_t.shape[1]
    blocks = rows // WIDE
    halves = rows // LANES
    row_i = lax.broadcasted_iota(jnp.int32, (LANES, LANES), 0)
    col_i = lax.broadcasted_iota(jnp.int32, (LANES, LANES), 1)
    causal = col_i >= row_i
    zero = jnp.zeros((LANES, LANES), BF16)
    time_down = lax.broadcasted_iota(jnp.int32, (WIDE, LANES), 0).astype(F32)
    time_along = lax.broadcasted_iota(jnp.int32, (LANES, WIDE), 1).astype(F32)
    lane_group = lax.broadcasted_iota(jnp.int32, (WIDE, LANES), 1) // MODES
    late = late_params[...]

    gated[0:8, :] = halo[LANES:LANES + 8, :].astype(F32) + halo[LANES + 8:LANES + 16, :].astype(F32)
    gated[8:24, :] = k[...].astype(F32) * v[...].astype(F32)
    total = late[0:1, :] * gated[8:24, :]
    for delay in range(1, SHORT):
        total = total + late[delay:delay + 1, :] * gated[8 - delay:24 - delay, :]
    opening = (q[...].astype(F32) * total).astype(BF16)
    opening = jnp.concatenate([opening, jnp.zeros((LANES - 16, LANES), BF16)], axis=0).T
    start[:, 0:LANES] = halo[0:LANES, :].T
    start[:, LANES:2 * LANES] = jnp.where(col_i < 16, opening, first_t[:, 0:LANES])

    def tile(chans, b):
        if b < 1:
            return start[chans, (b + 1) * LANES:(b + 2) * LANES]
        return first_t[chans, b * LANES:(b + 1) * LANES]

    def medium_of(g):
        chans = pl.ds(g * GROUP_CH, GROUP_CH)
        turned = jnp.broadcast_to(medium_taps[g:g + 1, :], (LANES, LANES))
        turned = pltpu.roll(turned, 0, 1, stride=1, stride_axis=0)
        medium_w = jnp.concatenate(
            [jnp.where(causal, 0.0, turned), jnp.where(causal, turned, 0.0)], axis=0).astype(BF16)
        window = jnp.concatenate([jnp.concatenate([tile(chans, b - 1), tile(chans, b)], axis=1) for b in range(halves)], axis=0)
        medium = jnp.dot(window, medium_w, preferred_element_type=F32)
        key = jnp.concatenate([key_t[chans, b * LANES:(b + 1) * LANES] for b in range(halves)], axis=0)
        second = (key.astype(F32) * medium).astype(BF16)
        for b in range(halves):
            seconds[(b // 2) * GROUP_CH:(b // 2 + 1) * GROUP_CH,
                    g * WIDE + (b % 2) * LANES:g * WIDE + (b % 2 + 1) * LANES] = (
                second[b * GROUP_CH:(b + 1) * GROUP_CH])

    for g in range(PACK):
        medium_of(g)

    rate = late[RATE:RATE + 1, :]
    tails = jnp.exp(-rate * (WIDE - 1.0 - time_down)).astype(BF16)
    tails_w = jnp.concatenate([jnp.where(lane_group == g, tails, jnp.zeros_like(tails)) for g in range(PACK)], axis=0)
    sums = jnp.dot(seconds[...], tails_w, preferred_element_type=F32)
    decay = jnp.exp(-rate * float(WIDE))
    state = jnp.zeros((GROUP_CH, LANES), F32)
    for b in range(blocks):
        carry_out[b * GROUP_CH:(b + 1) * GROUP_CH, :] = state
        state = decay * state + sums[b * GROUP_CH:(b + 1) * GROUP_CH, :]
    state_out[...] = state.astype(BF16)

    down = lambda row: jnp.broadcast_to(late[row:row + 1, :], (LANES, LANES)).T
    rate_t, amp_t, skip_t = down(RATE), down(AMP), down(SKIP)
    both = lambda half: jnp.concatenate([half, half], axis=1)
    power = both(amp_t) * jnp.exp(-both(rate_t) * time_along)

    def long_of(g):
        chans = pl.ds(g * GROUP_CH, GROUP_CH)
        mine = slice(g * MODES, (g + 1) * MODES)
        profile = jnp.sum(power[mine], axis=0, keepdims=True)
        turned = pltpu.roll(jnp.broadcast_to(profile, (LANES, WIDE)), 0, 1, stride=1, stride_axis=0)
        near = jnp.where(causal, turned[:, :LANES], 0.0).astype(BF16)
        pieces = [jnp.concatenate([near, turned[:, LANES:].astype(BF16)], axis=1),
                  jnp.concatenate([zero, near], axis=1)]
        second = seconds[:, g * WIDE:(g + 1) * WIDE]
        y = jnp.dot(second, jnp.concatenate(pieces, axis=0), preferred_element_type=F32)
        gain = both(skip_t[g * GROUP_CH:(g + 1) * GROUP_CH, :])
        gain = jnp.concatenate([gain] * blocks, axis=0)
        y = (y + gain * second.astype(F32)).astype(BF16)
        for b in range(blocks):
            y_t[chans, b * WIDE:(b + 1) * WIDE] = y[b * GROUP_CH:(b + 1) * GROUP_CH, :]

    for g in range(PACK):
        long_of(g)
    for begin in range(0, rows, LANES):
        y_out[pl.ds(begin, LANES), :] = y_t[:, begin:begin + LANES].T


def mix(first, keys_t, halo, q, k, v, params, medium_taps):
    chans, rows = first.shape
    column = lambda height: pl.BlockSpec((height, MIX_STRIP), lambda i: (0, i))
    down = lambda height, width: pl.BlockSpec((height, width), lambda i: (i, 0))
    carried = rows // WIDE * GROUP_CH
    return pl.pallas_call(
        mix_kernel,
        grid=(chans // MIX_STRIP,),
        out_shape=(jax.ShapeDtypeStruct((rows, chans), BF16), jax.ShapeDtypeStruct((carried, chans), F32),
                   jax.ShapeDtypeStruct((GROUP_CH, chans), BF16)),
        in_specs=[down(MIX_STRIP, rows)] * 2 + [column(halo.shape[0])] + [column(16)] * 3 + [
            column(params.shape[0]), down(MIX_STRIP // GROUP_CH, LANES)],
        out_specs=(column(rows), column(carried), column(GROUP_CH)),
        scratch_shapes=[
            pltpu.VMEM((LANES, rows), BF16),
            pltpu.VMEM((LANES, PACK * WIDE), BF16),
            pltpu.VMEM((24, LANES), F32),
            pltpu.VMEM((LANES, 2 * LANES), BF16),
        ] * (MIX_STRIP // LANES),
        compiler_params=pltpu.CompilerParams(vmem_limit_bytes=JOIN_VMEM),
        cost_estimate=pl.CostEstimate(flops=8 * rows * chans * WIDE, bytes_accessed=6 * rows * chans, transcendentals=0),
        name="mix",
    )(first, keys_t, halo, q, k, v, params, medium_taps)


def join_kernel(y, v, carry, states, weights, params, mixed_out, energy_out, energy):
    rows, wide = y.shape
    step = pl.program_id(0)

    @pl.when(step == 0)
    def _():
        energy[...] = jnp.zeros_like(energy)

    own = (lax.broadcasted_iota(jnp.int32, (WIDE, WIDE), 0) // GROUP_CH
           == lax.broadcasted_iota(jnp.int32, (WIDE, WIDE), 1) // MODES)
    time = lax.broadcasted_iota(jnp.int32, (WIDE, WIDE), 0).astype(F32) + 1.0
    nothing = jnp.zeros((WIDE, WIDE), BF16)
    entry = jnp.zeros((GROUP_CH, wide), F32)
    for source in range(states.shape[0]):
        entry = entry + weights[source:source + 1, :] * states[source].astype(F32)
    for s in range(wide // WIDE):
        here = slice(s * WIDE, (s + 1) * WIDE)
        rate = params[RATE:RATE + 1, here]
        lead = (params[AMP:AMP + 1, here] * jnp.exp(-rate * time)).astype(BF16)
        for b in range(rows // WIDE):
            part = pl.ds(b * WIDE, WIDE)
            state = carry[b * GROUP_CH:(b + 1) * GROUP_CH, here] + jnp.exp(-rate * float(b * WIDE)) * entry[:, here]
            spread = jnp.concatenate([state.astype(BF16)] * (WIDE // GROUP_CH), axis=0)
            carried = lax.dot_general(lead, jnp.where(own, spread, nothing), (((1,), (1,)), ((), ())),
                                      preferred_element_type=F32)
            mixed = v[part, here].astype(F32) * (y[part, here].astype(F32) + carried)
            mixed_out[part, here] = mixed.astype(BF16)
            square = mixed * mixed
            energy[part, :] += square[:, :LANES] + square[:, LANES:]

    @pl.when(step == pl.num_programs(0) - 1)
    def _():
        for begin in range(0, rows, LANES):
            energy_out[:, begin:begin + LANES] = jnp.sum(energy[pl.ds(begin, LANES), :].T, axis=0, keepdims=True)


def join(y, v, carry, states, weights, params):
    rows, chans = y.shape
    wide = math.gcd(chans, JOIN_STRIP)
    column = lambda height: pl.BlockSpec((height, wide), lambda i: (0, i))
    return pl.pallas_call(
        join_kernel,
        grid=(chans // wide,),
        out_shape=(jax.ShapeDtypeStruct((rows, chans), BF16), jax.ShapeDtypeStruct((1, rows), F32)),
        in_specs=[column(rows), column(rows), column(carry.shape[0]), pl.BlockSpec((states.shape[0], GROUP_CH, wide), lambda i: (0, 0, i)),
                  column(weights.shape[0]), column(params.shape[0])],
        out_specs=(column(rows), pl.BlockSpec((1, rows), lambda i: (0, 0))),
        scratch_shapes=[pltpu.VMEM((rows, LANES), F32)],
        compiler_params=pltpu.CompilerParams(vmem_limit_bytes=JOIN_VMEM),
        cost_estimate=pl.CostEstimate(flops=2 * rows * chans * WIDE, bytes_accessed=6 * rows * chans, transcendentals=0),
        name="join",
    )(y, v, carry, states, weights, params)


def scale_kernel(mixed, energy, gain, out, *, width):
    rows, chans = mixed.shape
    for begin in range(0, rows, LANES):
        part = pl.ds(begin, LANES)
        scale = jnp.sum(energy[:, begin:begin + LANES], axis=0, keepdims=True)
        scale = lax.rsqrt(scale / width + 1e-06)
        scale = jnp.broadcast_to(scale, (LANES, LANES)).T
        for left in range(0, chans, LANES):
            here = slice(left, left + LANES)
            out[part, here] = (mixed[part, here].astype(F32) * scale * gain[:, here]).astype(BF16)


def scaled(mixed, energy, gain, width):
    rows, chans = mixed.shape
    tall = math.gcd(rows, 512)
    block = pl.BlockSpec((tall, chans), lambda i: (i, 0))
    return pl.pallas_call(
        functools.partial(scale_kernel, width=width),
        grid=(rows // tall,),
        out_shape=jax.ShapeDtypeStruct((rows, chans), BF16),
        in_specs=[block, pl.BlockSpec((energy.shape[0], tall), lambda i: (0, i)), pl.BlockSpec((1, chans), lambda i: (0, 0))],
        out_specs=block,
        compiler_params=pltpu.CompilerParams(vmem_limit_bytes=JOIN_VMEM),
        name="scale",
    )(mixed, energy, gain)


def local(queries, key_rows, value_rows, short_filter, medium_filter, decays, residue, skip_gain,
          norm_gain, width):
    rows, chans = queries.shape
    queries, key_rows, value_rows = (pltpu.with_memory_space_constraint(array, pltpu.HBM)
                                     for array in (queries, key_rows, value_rows))
    amplitude = residue * jnp.sqrt(-jnp.expm1(-2.0 * decays))
    params = jnp.concatenate([
        jnp.repeat(short_filter, GROUP_CH, axis=1),
        decays.reshape(1, chans), amplitude.reshape(1, chans), skip_gain[None, :],
        jnp.zeros((16 - SHORT - 3, chans), F32)], axis=0)
    halo = passed_along(edge(queries, key_rows, value_rows, short_filter), "context", 1)
    first, keys_t = (pltpu.with_memory_space_constraint(array, pltpu.VMEM)
                     for array in gate(queries, key_rows, value_rows, params))
    y, carry, state = mix(first, keys_t, halo, queries, key_rows, value_rows, params, medium_filter.T.astype(F32))
    states = lax.all_gather(state, "context")
    count = lax.axis_size("context")
    gap = (lax.axis_index("context") - 1 - jnp.arange(count)).astype(F32)[:, None]
    weights = jnp.where(gap >= 0.0, jnp.exp(-params[RATE:RATE + 1] * (jnp.maximum(gap, 0.0) * rows)), 0.0)
    y = pltpu.with_memory_space_constraint(y, pltpu.VMEM)
    mixed, energy = join(y, value_rows, carry, states, weights, params)
    energy = summed(energy, "tensor")
    mixed = pltpu.with_memory_space_constraint(mixed, pltpu.VMEM)
    return scaled(mixed, energy, norm_gain[None, :], width)


def solution(mesh):
    def whole(*args):
        return jax.shard_map(
            functools.partial(local, width=args[0].shape[1]),
            mesh=mesh,
            in_specs=(
                P("context", "tensor"),
                P("context", "tensor"),
                P("context", "tensor"),
                P(None, "tensor"),
                P(None, "tensor"),
                P("tensor", None),
                P("tensor", None),
                P("tensor"),
                P("tensor"),
            ),
            out_specs=P("context", "tensor"),
            check_vma=False,
        )(*args)

    return whole
```

```python
import functools
import math

import jax
import jax.numpy as jnp
from jax import lax
from jax.experimental import pallas as pl
from jax.experimental.pallas import tpu as pltpu
from jax.sharding import PartitionSpec as P

GROUP_CH = 16
LANES = 128
PACK = LANES // GROUP_CH
WIDE = 256
MODES = 16
SHORT = 7
RATE, AMP, SKIP = SHORT, SHORT + 1, SHORT + 2
GATE_STRIP = 256
MIX_STRIP = 256
JOIN_STRIP = 512
MIX_VMEM = 24 << 20
JOIN_VMEM = 24 << 20
F32 = jnp.float32
BF16 = jnp.bfloat16


def split2(value):
    high = value.astype(BF16)
    return high, (value - high.astype(F32)).astype(BF16)


def passed_along(value, axis, steps):
    count = lax.axis_size(axis)
    return lax.ppermute(value, axis, [(source, source + steps) for source in range(count - steps)])


def edge_kernel(q, k, v, short_filter, halo_out, q_tail, k_tail, v_tail, gated, arrived):
    rows, chans = q.shape
    parts = arrived.shape[0]
    wide = chans // parts
    pack = wide // GROUP_CH
    tail = LANES + 16
    copies = []
    for s in range(parts):
        here = pl.ds(s * wide, wide)
        copies.append([pltpu.make_async_copy(source.at[pl.ds(rows - tail, tail), here], target.at[:, here], arrived.at[s, n])
                       for n, (source, target) in enumerate(((q, q_tail), (k, k_tail), (v, v_tail)))])
        for copy in copies[-1]:
            copy.start()
    spread = (lax.broadcasted_iota(jnp.int32, (pack, wide), 1) // GROUP_CH
              == lax.broadcasted_iota(jnp.int32, (pack, wide), 0)).astype(F32)
    for s in range(parts):
        here = pl.ds(s * wide, wide)
        taps = jnp.dot(short_filter[:, s * pack:(s + 1) * pack], spread, precision=lax.Precision.HIGHEST,
                       preferred_element_type=F32)
        for copy in copies[s]:
            copy.wait()
        kv = k_tail[:, here].astype(F32) * v_tail[:, here].astype(F32)
        gated[...] = kv
        total = taps[0:1, :] * kv[16:, :]
        for delay in range(1, SHORT):
            total = total + taps[delay:delay + 1, :] * gated[pl.ds(16 - delay, LANES), :]
        halo_out[0:LANES, here] = (q_tail[16:, here].astype(F32) * total).astype(BF16)
        last = kv[LANES + 8:, :]
        high = last.astype(BF16).astype(F32)
        halo_out[LANES:LANES + 16, here] = jnp.concatenate([high, last - high], axis=0).astype(BF16)


def edge(q, k, v, short_filter):
    chans = q.shape[1]
    parts = chans // math.gcd(chans, 512)
    far = pl.BlockSpec(memory_space=pltpu.HBM)
    return pl.pallas_call(
        edge_kernel,
        out_shape=jax.ShapeDtypeStruct((LANES + 16, chans), BF16),
        in_specs=[far] * 3 + [pl.BlockSpec(memory_space=pltpu.VMEM)],
        out_specs=pl.BlockSpec(memory_space=pltpu.VMEM),
        scratch_shapes=[pltpu.VMEM((LANES + 16, chans), BF16)] * 3 + [
            pltpu.VMEM((LANES + 16, chans // parts), F32), pltpu.SemaphoreType.DMA((parts, 3))],
        compiler_params=pltpu.CompilerParams(vmem_limit_bytes=MIX_VMEM),
        name="edge",
    )(q, k, v, short_filter)


def gate_kernel(q, k, v, params, first_out, key_out, *gated_refs):
    rows, wide = q.shape
    for s, gated in enumerate(gated_refs):
        here = slice(s * LANES, (s + 1) * LANES)
        taps = params[:, here]
        gated[0:8, :] = jnp.zeros((8, LANES), F32)
        for begin in range(0, rows, LANES):
            part = pl.ds(begin, LANES)
            keys = k[part, here]
            fresh = keys.astype(F32) * v[part, here].astype(F32)
            gated[pl.ds(begin + 8, LANES), :] = fresh
            total = taps[0:1, :] * fresh
            for delay in range(1, SHORT):
                total = total + taps[delay:delay + 1, :] * gated[pl.ds(begin + 8 - delay, LANES), :]
            first = (q[part, here].astype(F32) * total).astype(BF16)
            first_out[here, begin:begin + LANES] = first.T
            key_out[here, begin:begin + LANES] = keys.T


def gate(q, k, v, params):
    rows, chans = q.shape
    column = lambda height: pl.BlockSpec((height, GATE_STRIP), lambda i: (0, i))
    down = pl.BlockSpec((GATE_STRIP, rows), lambda i: (i, 0))
    return pl.pallas_call(
        gate_kernel,
        grid=(chans // GATE_STRIP,),
        out_shape=(jax.ShapeDtypeStruct((chans, rows), BF16),) * 2,
        in_specs=[column(rows)] * 3 + [column(params.shape[0])],
        out_specs=(down, down),
        scratch_shapes=[pltpu.VMEM((rows + 8, LANES), F32)] * (GATE_STRIP // LANES),
        compiler_params=pltpu.CompilerParams(vmem_limit_bytes=MIX_VMEM),
        cost_estimate=pl.CostEstimate(flops=64 * rows * chans, bytes_accessed=10 * rows * chans, transcendentals=0),
        name="gate",
    )(q, k, v, params)


def summed(value, axis):
    count = lax.axis_size(axis)
    if count & (count - 1):
        return lax.psum(value, axis)
    step = 1
    while step < count:
        value = value + lax.ppermute(value, axis, [(source, source ^ step) for source in range(count)])
        step *= 2
    return value


def mix_kernel(first, keys_t, halo, q, k, v, params, medium_taps, seconds_out, carry_out, state_out, *scratch):
    strips = first.shape[0] // LANES
    for s in range(strips):
        here = slice(s * LANES, (s + 1) * LANES)
        mix_strip(first.at[here, :], keys_t.at[here, :], halo.at[:, here], q.at[:, here], k.at[:, here], v.at[:, here],
                  params.at[:, here], medium_taps.at[s * PACK:(s + 1) * PACK, :],
                  seconds_out.at[here, :], carry_out.at[:, here], state_out.at[:, here], *scratch[2 * s:2 * s + 2])


def mix_strip(first_t, key_t, halo, q, k, v, late_params, medium_taps, seconds, carry_out, state_out,
              gated, start):
    rows = first_t.shape[1]
    blocks = rows // WIDE
    halves = rows // LANES
    row_i = lax.broadcasted_iota(jnp.int32, (LANES, LANES), 0)
    col_i = lax.broadcasted_iota(jnp.int32, (LANES, LANES), 1)
    causal = col_i >= row_i
    time_down = lax.broadcasted_iota(jnp.int32, (WIDE, LANES), 0).astype(F32)
    lane_group = lax.broadcasted_iota(jnp.int32, (WIDE, LANES), 1) // MODES
    late = late_params[...]

    gated[0:8, :] = halo[LANES:LANES + 8, :].astype(F32) + halo[LANES + 8:LANES + 16, :].astype(F32)
    gated[8:24, :] = k[...].astype(F32) * v[...].astype(F32)
    total = late[0:1, :] * gated[8:24, :]
    for delay in range(1, SHORT):
        total = total + late[delay:delay + 1, :] * gated[8 - delay:24 - delay, :]
    opening = (q[...].astype(F32) * total).astype(BF16)
    opening = jnp.concatenate([opening, jnp.zeros((LANES - 16, LANES), BF16)], axis=0).T
    start[:, 0:LANES] = halo[0:LANES, :].T
    start[:, LANES:2 * LANES] = jnp.where(col_i < 16, opening, first_t[:, 0:LANES])

    def tile(chans, b):
        if b < 1:
            return start[chans, (b + 1) * LANES:(b + 2) * LANES]
        return first_t[chans, b * LANES:(b + 1) * LANES]

    def medium_of(g):
        chans = pl.ds(g * GROUP_CH, GROUP_CH)
        turned = jnp.broadcast_to(medium_taps[g:g + 1, :], (LANES, LANES))
        turned = pltpu.roll(turned, 0, 1, stride=1, stride_axis=0)
        medium_w = jnp.concatenate(
            [jnp.where(causal, 0.0, turned), jnp.where(causal, turned, 0.0)], axis=0).astype(BF16)
        window = jnp.concatenate([jnp.concatenate([tile(chans, b - 1), tile(chans, b)], axis=1) for b in range(halves)], axis=0)
        medium = jnp.dot(window, medium_w, preferred_element_type=F32)
        key = jnp.concatenate([key_t[chans, b * LANES:(b + 1) * LANES] for b in range(halves)], axis=0)
        second = (key.astype(F32) * medium).astype(BF16)
        for b in range(halves):
            seconds[(b // 2) * GROUP_CH:(b // 2 + 1) * GROUP_CH,
                    g * WIDE + (b % 2) * LANES:g * WIDE + (b % 2 + 1) * LANES] = (
                second[b * GROUP_CH:(b + 1) * GROUP_CH])

    for g in range(PACK):
        medium_of(g)

    rate = late[RATE:RATE + 1, :]
    tails = jnp.exp(-rate * (WIDE - 1.0 - time_down)).astype(BF16)
    tails_w = jnp.concatenate([jnp.where(lane_group == g, tails, jnp.zeros_like(tails)) for g in range(PACK)], axis=0)
    sums = jnp.dot(seconds[...], tails_w, preferred_element_type=F32)
    decay = jnp.exp(-rate * float(WIDE))
    state = jnp.zeros((GROUP_CH, LANES), F32)
    for b in range(blocks):
        carry_out[b * GROUP_CH:(b + 1) * GROUP_CH, :] = state
        state = decay * state + sums[b * GROUP_CH:(b + 1) * GROUP_CH, :]
    state_out[...] = state.astype(BF16)


def long_kernel(seconds, params, y_out, *scratch):
    for s in range(seconds.shape[0] // LANES):
        here = slice(s * LANES, (s + 1) * LANES)
        long_strip(seconds.at[here, :], params.at[:, here], y_out.at[:, here], scratch[s])


def long_strip(seconds, params, y_out, y_t):
    rows = y_out.shape[0]
    blocks = rows // WIDE
    row_i = lax.broadcasted_iota(jnp.int32, (LANES, LANES), 0)
    col_i = lax.broadcasted_iota(jnp.int32, (LANES, LANES), 1)
    causal = col_i >= row_i
    zero = jnp.zeros((LANES, LANES), BF16)
    time_along = lax.broadcasted_iota(jnp.int32, (LANES, WIDE), 1).astype(F32)
    late = params[...]

    down = lambda row: jnp.broadcast_to(late[row:row + 1, :], (LANES, LANES)).T
    rate_t, amp_t, skip_t = down(RATE), down(AMP), down(SKIP)
    both = lambda half: jnp.concatenate([half, half], axis=1)
    power = both(amp_t) * jnp.exp(-both(rate_t) * time_along)

    def long_of(g):
        chans = pl.ds(g * GROUP_CH, GROUP_CH)
        mine = slice(g * MODES, (g + 1) * MODES)
        profile = jnp.sum(power[mine], axis=0, keepdims=True)
        turned = pltpu.roll(jnp.broadcast_to(profile, (LANES, WIDE)), 0, 1, stride=1, stride_axis=0)
        near = jnp.where(causal, turned[:, :LANES], 0.0).astype(BF16)
        pieces = [jnp.concatenate([near, turned[:, LANES:].astype(BF16)], axis=1),
                  jnp.concatenate([zero, near], axis=1)]
        second = seconds[:, g * WIDE:(g + 1) * WIDE]
        y = jnp.dot(second, jnp.concatenate(pieces, axis=0), preferred_element_type=F32)
        gain = both(skip_t[g * GROUP_CH:(g + 1) * GROUP_CH, :])
        gain = jnp.concatenate([gain] * blocks, axis=0)
        y = (y + gain * second.astype(F32)).astype(BF16)
        for b in range(blocks):
            y_t[chans, b * WIDE:(b + 1) * WIDE] = y[b * GROUP_CH:(b + 1) * GROUP_CH, :]

    for g in range(PACK):
        long_of(g)
    for begin in range(0, rows, LANES):
        y_out[pl.ds(begin, LANES), :] = y_t[:, begin:begin + LANES].T


def mix(first, keys_t, halo, q, k, v, params, medium_taps):
    chans, rows = first.shape
    column = lambda height: pl.BlockSpec((height, MIX_STRIP), lambda i: (0, i))
    down = lambda height, width: pl.BlockSpec((height, width), lambda i: (i, 0))
    carried = rows // WIDE * GROUP_CH
    return pl.pallas_call(
        mix_kernel,
        grid=(chans // MIX_STRIP,),
        out_shape=(pltpu.HBM((chans, rows), BF16), jax.ShapeDtypeStruct((carried, chans), F32),
                   jax.ShapeDtypeStruct((GROUP_CH, chans), BF16)),
        in_specs=[down(MIX_STRIP, rows)] * 2 + [column(halo.shape[0])] + [column(16)] * 3 + [
            column(params.shape[0]), down(MIX_STRIP // GROUP_CH, LANES)],
        out_specs=(down(MIX_STRIP, rows), column(carried), column(GROUP_CH)),
        scratch_shapes=[pltpu.VMEM((24, LANES), F32), pltpu.VMEM((LANES, 2 * LANES), BF16)] * (MIX_STRIP // LANES),
        compiler_params=pltpu.CompilerParams(vmem_limit_bytes=MIX_VMEM),
        cost_estimate=pl.CostEstimate(flops=6 * rows * chans * WIDE, bytes_accessed=6 * rows * chans, transcendentals=0),
        name="mix",
    )(first, keys_t, halo, q, k, v, params, medium_taps)


def long_conv(seconds, params):
    chans, rows = seconds.shape
    column = lambda height: pl.BlockSpec((height, MIX_STRIP), lambda i: (0, i))
    return pl.pallas_call(
        long_kernel,
        grid=(chans // MIX_STRIP,),
        out_shape=jax.ShapeDtypeStruct((rows, chans), BF16),
        in_specs=[pl.BlockSpec((MIX_STRIP, rows), lambda i: (i, 0)), column(params.shape[0])],
        out_specs=column(rows),
        scratch_shapes=[pltpu.VMEM((LANES, rows), BF16)] * (MIX_STRIP // LANES),
        compiler_params=pltpu.CompilerParams(vmem_limit_bytes=MIX_VMEM),
        cost_estimate=pl.CostEstimate(flops=6 * rows * chans * WIDE, bytes_accessed=10 * rows * chans, transcendentals=0),
        name="long",
    )(seconds, params)


def join_kernel(y, v, carry, entry, params, mixed_out, energy_out, energy):
    rows, wide = y.shape
    step = pl.program_id(0)

    @pl.when(step == 0)
    def _():
        energy[...] = jnp.zeros_like(energy)

    own = (lax.broadcasted_iota(jnp.int32, (WIDE, WIDE), 0) // GROUP_CH
           == lax.broadcasted_iota(jnp.int32, (WIDE, WIDE), 1) // MODES)
    time = lax.broadcasted_iota(jnp.int32, (WIDE, WIDE), 0).astype(F32) + 1.0
    nothing = jnp.zeros((WIDE, WIDE), BF16)
    for s in range(wide // WIDE):
        here = slice(s * WIDE, (s + 1) * WIDE)
        rate = params[RATE:RATE + 1, here]
        lead = (params[AMP:AMP + 1, here] * jnp.exp(-rate * time)).astype(BF16)
        for b in range(rows // WIDE):
            part = pl.ds(b * WIDE, WIDE)
            state = carry[b * GROUP_CH:(b + 1) * GROUP_CH, here] + jnp.exp(-rate * float(b * WIDE)) * entry[:, here]
            spread = jnp.concatenate([state.astype(BF16)] * (WIDE // GROUP_CH), axis=0)
            carried = lax.dot_general(lead, jnp.where(own, spread, nothing), (((1,), (1,)), ((), ())),
                                      preferred_element_type=F32)
            mixed = v[part, here].astype(F32) * (y[part, here].astype(F32) + carried)
            mixed_out[part, here] = mixed.astype(BF16)
            square = mixed * mixed
            energy[part, :] += square[:, :LANES] + square[:, LANES:]

    @pl.when(step == pl.num_programs(0) - 1)
    def _():
        for begin in range(0, rows, LANES):
            energy_out[:, begin:begin + LANES] = jnp.sum(energy[pl.ds(begin, LANES), :].T, axis=0, keepdims=True)


def join(y, v, carry, entry, params):
    rows, chans = y.shape
    wide = math.gcd(chans, JOIN_STRIP)
    column = lambda height: pl.BlockSpec((height, wide), lambda i: (0, i))
    return pl.pallas_call(
        join_kernel,
        grid=(chans // wide,),
        out_shape=(jax.ShapeDtypeStruct((rows, chans), BF16), jax.ShapeDtypeStruct((1, rows), F32)),
        in_specs=[column(rows), column(rows), column(carry.shape[0]),
                  column(GROUP_CH), column(params.shape[0])],
        out_specs=(column(rows), pl.BlockSpec((1, rows), lambda i: (0, 0))),
        scratch_shapes=[pltpu.VMEM((rows, LANES), F32)],
        compiler_params=pltpu.CompilerParams(vmem_limit_bytes=JOIN_VMEM),
        cost_estimate=pl.CostEstimate(flops=2 * rows * chans * WIDE, bytes_accessed=6 * rows * chans, transcendentals=0),
        name="join",
    )(y, v, carry, entry, params)


def scale_kernel(mixed, energy, gain, out, *, width):
    rows, chans = mixed.shape
    for begin in range(0, rows, LANES):
        part = pl.ds(begin, LANES)
        scale = jnp.sum(energy[:, begin:begin + LANES], axis=0, keepdims=True)
        scale = lax.rsqrt(scale / width + 1e-06)
        scale = jnp.broadcast_to(scale, (LANES, LANES)).T
        for left in range(0, chans, LANES):
            here = slice(left, left + LANES)
            out[part, here] = (mixed[part, here].astype(F32) * scale * gain[:, here]).astype(BF16)


def scaled(mixed, energy, gain, width):
    rows, chans = mixed.shape
    tall = math.gcd(rows, 512)
    block = pl.BlockSpec((tall, chans), lambda i: (i, 0))
    return pl.pallas_call(
        functools.partial(scale_kernel, width=width),
        grid=(rows // tall,),
        out_shape=jax.ShapeDtypeStruct((rows, chans), BF16),
        in_specs=[block, pl.BlockSpec((energy.shape[0], tall), lambda i: (0, i)), pl.BlockSpec((1, chans), lambda i: (0, 0))],
        out_specs=block,
        compiler_params=pltpu.CompilerParams(vmem_limit_bytes=JOIN_VMEM),
        name="scale",
    )(mixed, energy, gain)


def local(queries, key_rows, value_rows, short_filter, medium_filter, decays, residue, skip_gain,
          norm_gain, width):
    rows, chans = queries.shape
    queries, key_rows, value_rows = (pltpu.with_memory_space_constraint(array, pltpu.HBM)
                                     for array in (queries, key_rows, value_rows))
    amplitude = residue * jnp.sqrt(-jnp.expm1(-2.0 * decays))
    params = jnp.concatenate([
        jnp.repeat(short_filter, GROUP_CH, axis=1),
        decays.reshape(1, chans), amplitude.reshape(1, chans), skip_gain[None, :],
        jnp.zeros((16 - SHORT - 3, chans), F32)], axis=0)
    halo = passed_along(edge(queries, key_rows, value_rows, short_filter), "context", 1)
    first, keys_t = (pltpu.with_memory_space_constraint(array, pltpu.VMEM)
                     for array in gate(queries, key_rows, value_rows, params))
    seconds, carry, state = mix(first, keys_t, halo, queries, key_rows, value_rows, params, medium_filter.T.astype(F32))
    entry = jnp.zeros(state.shape, F32)
    for away in range(1, lax.axis_size("context")):
        fade = jnp.exp(-params[RATE:RATE + 1] * float(rows * (away - 1)))
        entry = entry + fade * passed_along(state, "context", away).astype(F32)
    y = long_conv(pltpu.with_memory_space_constraint(seconds, pltpu.HBM), params)
    y = pltpu.with_memory_space_constraint(y, pltpu.VMEM)
    mixed, energy = join(y, value_rows, carry, entry, params)
    energy = summed(energy, "tensor")
    mixed = pltpu.with_memory_space_constraint(mixed, pltpu.VMEM)
    return scaled(mixed, energy, norm_gain[None, :], width)


def solution(mesh):
    def whole(*args):
        return jax.shard_map(
            functools.partial(local, width=args[0].shape[1]),
            mesh=mesh,
            in_specs=(
                P("context", "tensor"),
                P("context", "tensor"),
                P("context", "tensor"),
                P(None, "tensor"),
                P(None, "tensor"),
                P("tensor", None),
                P("tensor", None),
                P("tensor"),
                P("tensor"),
            ),
            out_specs=P("context", "tensor"),
            check_vma=False,
        )(*args)

    return whole
```

```python
import functools
import math

import jax
import jax.numpy as jnp
from jax import lax
from jax.experimental import pallas as pl
from jax.experimental.pallas import tpu as pltpu
from jax.sharding import PartitionSpec as P

GROUP_CH = 16
LANES = 128
PACK = LANES // GROUP_CH
WIDE = 256
MODES = 16
SHORT = 7
RATE, AMP, SKIP = SHORT, SHORT + 1, SHORT + 2
GATE_STRIP = 256
MIX_STRIP = 512
EDGE_PARTS = 1
JOIN_STRIP = 512
MIX_VMEM = 24 << 20
JOIN_VMEM = 24 << 20
F32 = jnp.float32
BF16 = jnp.bfloat16


def split2(value):
    high = value.astype(BF16)
    return high, (value - high.astype(F32)).astype(BF16)


def passed_along(value, axis, steps):
    count = lax.axis_size(axis)
    return lax.ppermute(value, axis, [(source, source + steps) for source in range(count - steps)])


def edge_kernel(q, k, v, short_filter, halo_out, gated):
    rows, wide = q.shape
    begin = rows - LANES
    pack = wide // GROUP_CH
    spread = (lax.broadcasted_iota(jnp.int32, (pack, wide), 1) // GROUP_CH
              == lax.broadcasted_iota(jnp.int32, (pack, wide), 0)).astype(F32)
    taps = jnp.dot(short_filter[...], spread, precision=lax.Precision.HIGHEST, preferred_element_type=F32)
    kv = k[begin - 16:, :].astype(F32) * v[begin - 16:, :].astype(F32)
    gated[...] = kv
    total = taps[0:1, :] * gated[16:, :]
    for delay in range(1, SHORT):
        total = total + taps[delay:delay + 1, :] * gated[pl.ds(16 - delay, LANES), :]
    halo_out[0:LANES, :] = (q[begin:, :].astype(F32) * total).astype(BF16)
    last = kv[LANES + 8:, :]
    high = last.astype(BF16).astype(F32)
    halo_out[LANES:LANES + 16, :] = jnp.concatenate([high, last - high], axis=0).astype(BF16)


def edge(q, k, v, short_filter):
    rows, chans = q.shape
    wide = chans // EDGE_PARTS
    tall = math.gcd(rows, 256)
    last = pl.BlockSpec((tall, wide), lambda i: (rows // tall - 1, i))
    column = lambda height, width: pl.BlockSpec((height, width), lambda i: (0, i))
    if EDGE_PARTS > 1 and wide // GROUP_CH % LANES:
        short_filter = short_filter.reshape(SHORT, EDGE_PARTS, wide // GROUP_CH).transpose(1, 0, 2)
        tap_spec = pl.BlockSpec((pl.Squeezed(), SHORT, wide // GROUP_CH), lambda i: (i, 0, 0))
    else:
        tap_spec = column(SHORT, wide // GROUP_CH)
    return pl.pallas_call(
        edge_kernel,
        grid=(EDGE_PARTS,),
        out_shape=jax.ShapeDtypeStruct((LANES + 16, chans), BF16),
        in_specs=[last] * 3 + [tap_spec],
        out_specs=column(LANES + 16, wide),
        scratch_shapes=[pltpu.VMEM((LANES + 16, wide), F32)],
        compiler_params=pltpu.CompilerParams(vmem_limit_bytes=MIX_VMEM),
        name="edge",
    )(q, k, v, short_filter)


def gate_kernel(q, k, v, params, first_out, key_out, *gated_refs):
    rows, wide = q.shape
    for s, gated in enumerate(gated_refs):
        here = slice(s * LANES, (s + 1) * LANES)
        taps = params[:, here]
        gated[0:8, :] = jnp.zeros((8, LANES), F32)
        for begin in range(0, rows, LANES):
            part = pl.ds(begin, LANES)
            keys = k[part, here]
            fresh = keys.astype(F32) * v[part, here].astype(F32)
            gated[pl.ds(begin + 8, LANES), :] = fresh
            total = taps[0:1, :] * fresh
            for delay in range(1, SHORT):
                total = total + taps[delay:delay + 1, :] * gated[pl.ds(begin + 8 - delay, LANES), :]
            first = (q[part, here].astype(F32) * total).astype(BF16)
            first_out[here, begin:begin + LANES] = first.T
            key_out[here, begin:begin + LANES] = keys.T


def gate(q, k, v, params):
    rows, chans = q.shape
    column = lambda height: pl.BlockSpec((height, GATE_STRIP), lambda i: (0, i))
    down = pl.BlockSpec((GATE_STRIP, rows), lambda i: (i, 0))
    return pl.pallas_call(
        gate_kernel,
        grid=(chans // GATE_STRIP,),
        out_shape=(jax.ShapeDtypeStruct((chans, rows), BF16),) * 2,
        in_specs=[column(rows)] * 3 + [column(params.shape[0])],
        out_specs=(down, down),
        scratch_shapes=[pltpu.VMEM((rows + 8, LANES), F32)] * (GATE_STRIP // LANES),
        compiler_params=pltpu.CompilerParams(vmem_limit_bytes=MIX_VMEM),
        cost_estimate=pl.CostEstimate(flops=64 * rows * chans, bytes_accessed=10 * rows * chans, transcendentals=0),
        name="gate",
    )(q, k, v, params)


def summed(value, axis):
    count = lax.axis_size(axis)
    if count & (count - 1):
        return lax.psum(value, axis)
    step = 1
    while step < count:
        value = value + lax.ppermute(value, axis, [(source, source ^ step) for source in range(count)])
        step *= 2
    return value


def mix_kernel(first, keys_t, halo, q, k, v, params, medium_taps, y_out, carry_out, state_out, *scratch):
    strips = first.shape[0] // LANES
    for s in range(strips):
        here = slice(s * LANES, (s + 1) * LANES)
        mix_strip(first.at[here, :], keys_t.at[here, :], halo.at[:, here], q.at[:, here], k.at[:, here], v.at[:, here],
                  params.at[:, here], medium_taps.at[s * PACK:(s + 1) * PACK, :],
                  y_out.at[:, here], carry_out.at[:, here], state_out.at[:, here], *scratch[4 * s:4 * s + 4])


def mix_strip(first_t, key_t, halo, q, k, v, late_params, medium_taps, y_out, carry_out, state_out, y_t, seconds,
              gated, start):
    rows = first_t.shape[1]
    blocks = rows // WIDE
    halves = rows // LANES
    row_i = lax.broadcasted_iota(jnp.int32, (LANES, LANES), 0)
    col_i = lax.broadcasted_iota(jnp.int32, (LANES, LANES), 1)
    causal = col_i >= row_i
    zero = jnp.zeros((LANES, LANES), BF16)
    time_down = lax.broadcasted_iota(jnp.int32, (WIDE, LANES), 0).astype(F32)
    time_along = lax.broadcasted_iota(jnp.int32, (LANES, WIDE), 1).astype(F32)
    lane_group = lax.broadcasted_iota(jnp.int32, (WIDE, LANES), 1) // MODES
    late = late_params[...]

    gated[0:8, :] = halo[LANES:LANES + 8, :].astype(F32) + halo[LANES + 8:LANES + 16, :].astype(F32)
    gated[8:24, :] = k[...].astype(F32) * v[...].astype(F32)
    total = late[0:1, :] * gated[8:24, :]
    for delay in range(1, SHORT):
        total = total + late[delay:delay + 1, :] * gated[8 - delay:24 - delay, :]
    opening = (q[...].astype(F32) * total).astype(BF16)
    opening = jnp.concatenate([opening, jnp.zeros((LANES - 16, LANES), BF16)], axis=0).T
    start[:, 0:LANES] = halo[0:LANES, :].T
    start[:, LANES:2 * LANES] = jnp.where(col_i < 16, opening, first_t[:, 0:LANES])

    def tile(chans, b):
        if b < 1:
            return start[chans, (b + 1) * LANES:(b + 2) * LANES]
        return first_t[chans, b * LANES:(b + 1) * LANES]

    def medium_of(g):
        chans = pl.ds(g * GROUP_CH, GROUP_CH)
        turned = jnp.broadcast_to(medium_taps[g:g + 1, :], (LANES, LANES))
        turned = pltpu.roll(turned, 0, 1, stride=1, stride_axis=0)
        medium_w = jnp.concatenate(
            [jnp.where(causal, 0.0, turned), jnp.where(causal, turned, 0.0)], axis=0).astype(BF16)
        window = jnp.concatenate([jnp.concatenate([tile(chans, b - 1), tile(chans, b)], axis=1) for b in range(halves)], axis=0)
        medium = jnp.dot(window, medium_w, preferred_element_type=F32)
        key = jnp.concatenate([key_t[chans, b * LANES:(b + 1) * LANES] for b in range(halves)], axis=0)
        second = (key.astype(F32) * medium).astype(BF16)
        for b in range(halves):
            seconds[(b // 2) * GROUP_CH:(b // 2 + 1) * GROUP_CH,
                    g * WIDE + (b % 2) * LANES:g * WIDE + (b % 2 + 1) * LANES] = (
                second[b * GROUP_CH:(b + 1) * GROUP_CH])

    for g in range(PACK):
        medium_of(g)

    rate = late[RATE:RATE + 1, :]
    tails = jnp.exp(-rate * (WIDE - 1.0 - time_down)).astype(BF16)
    tails_w = jnp.concatenate([jnp.where(lane_group == g, tails, jnp.zeros_like(tails)) for g in range(PACK)], axis=0)
    sums = jnp.dot(seconds[...], tails_w, preferred_element_type=F32)
    decay = jnp.exp(-rate * float(WIDE))
    state = jnp.zeros((GROUP_CH, LANES), F32)
    for b in range(blocks):
        carry_out[b * GROUP_CH:(b + 1) * GROUP_CH, :] = state
        state = decay * state + sums[b * GROUP_CH:(b + 1) * GROUP_CH, :]
    state_out[...] = state.astype(BF16)

    down = lambda row: jnp.broadcast_to(late[row:row + 1, :], (LANES, LANES)).T
    rate_t, amp_t, skip_t = down(RATE), down(AMP), down(SKIP)
    both = lambda half: jnp.concatenate([half, half], axis=1)
    power = both(amp_t) * jnp.exp(-both(rate_t) * time_along)

    def long_of(g):
        chans = pl.ds(g * GROUP_CH, GROUP_CH)
        mine = slice(g * MODES, (g + 1) * MODES)
        profile = jnp.sum(power[mine], axis=0, keepdims=True)
        soon, late_part = (
            pltpu.roll(jnp.broadcast_to(profile[:, half * LANES:(half + 1) * LANES], (LANES, LANES)),
                       0, 1, stride=1, stride_axis=0) for half in range(2))
        near = jnp.where(causal, soon, 0.0).astype(BF16)
        far = jnp.where(causal, late_part, soon).astype(BF16)
        pieces = [jnp.concatenate([near, far], axis=1), jnp.concatenate([zero, near], axis=1)]
        second = seconds[:, g * WIDE:(g + 1) * WIDE]
        y = jnp.dot(second, jnp.concatenate(pieces, axis=0), preferred_element_type=F32)
        gain = both(skip_t[g * GROUP_CH:(g + 1) * GROUP_CH, :])
        gain = jnp.concatenate([gain] * blocks, axis=0)
        y = (y + gain * second.astype(F32)).astype(BF16)
        for b in range(blocks):
            y_t[chans, b * WIDE:(b + 1) * WIDE] = y[b * GROUP_CH:(b + 1) * GROUP_CH, :]

    for g in range(PACK):
        long_of(g)
    for begin in range(0, rows, LANES):
        y_out[pl.ds(begin, LANES), :] = y_t[:, begin:begin + LANES].T


def mix(first, keys_t, halo, q, k, v, params, medium_taps):
    chans, rows = first.shape
    column = lambda height: pl.BlockSpec((height, MIX_STRIP), lambda i: (0, i))
    down = lambda height, width: pl.BlockSpec((height, width), lambda i: (i, 0))
    carried = rows // WIDE * GROUP_CH
    return pl.pallas_call(
        mix_kernel,
        grid=(chans // MIX_STRIP,),
        out_shape=(jax.ShapeDtypeStruct((rows, chans), BF16), jax.ShapeDtypeStruct((carried, chans), F32),
                   jax.ShapeDtypeStruct((GROUP_CH, chans), BF16)),
        in_specs=[down(MIX_STRIP, rows)] * 2 + [column(halo.shape[0])] + [column(16)] * 3 + [
            column(params.shape[0]), down(MIX_STRIP // GROUP_CH, LANES)],
        out_specs=(column(rows), column(carried), column(GROUP_CH)),
        scratch_shapes=[
            pltpu.VMEM((LANES, rows), BF16),
            pltpu.VMEM((LANES, PACK * WIDE), BF16),
            pltpu.VMEM((24, LANES), F32),
            pltpu.VMEM((LANES, 2 * LANES), BF16),
        ] * (MIX_STRIP // LANES),
        compiler_params=pltpu.CompilerParams(vmem_limit_bytes=JOIN_VMEM),
        cost_estimate=pl.CostEstimate(flops=8 * rows * chans * WIDE, bytes_accessed=6 * rows * chans, transcendentals=0),
        name="mix",
    )(first, keys_t, halo, q, k, v, params, medium_taps)


def join_kernel(y, v, carry, states, weights, params, mixed_out, energy_out, energy):
    rows, wide = y.shape
    step = pl.program_id(0)

    @pl.when(step == 0)
    def _():
        energy[...] = jnp.zeros_like(energy)

    own = (lax.broadcasted_iota(jnp.int32, (WIDE, WIDE), 0) // GROUP_CH
           == lax.broadcasted_iota(jnp.int32, (WIDE, WIDE), 1) // MODES)
    time = lax.broadcasted_iota(jnp.int32, (WIDE, WIDE), 0).astype(F32) + 1.0
    nothing = jnp.zeros((WIDE, WIDE), BF16)
    entry = jnp.zeros((GROUP_CH, wide), F32)
    for source in range(states.shape[0]):
        entry = entry + weights[source:source + 1, :] * states[source].astype(F32)
    for s in range(wide // WIDE):
        here = slice(s * WIDE, (s + 1) * WIDE)
        rate = params[RATE:RATE + 1, here]
        lead = (params[AMP:AMP + 1, here] * jnp.exp(-rate * time)).astype(BF16)
        for b in range(rows // WIDE):
            part = pl.ds(b * WIDE, WIDE)
            state = carry[b * GROUP_CH:(b + 1) * GROUP_CH, here] + jnp.exp(-rate * float(b * WIDE)) * entry[:, here]
            spread = jnp.concatenate([state.astype(BF16)] * (WIDE // GROUP_CH), axis=0)
            carried = lax.dot_general(lead, jnp.where(own, spread, nothing), (((1,), (1,)), ((), ())),
                                      preferred_element_type=F32)
            mixed = v[part, here].astype(F32) * (y[part, here].astype(F32) + carried)
            mixed_out[part, here] = mixed.astype(BF16)
            square = mixed * mixed
            energy[part, :] += square[:, :LANES] + square[:, LANES:]

    @pl.when(step == pl.num_programs(0) - 1)
    def _():
        for begin in range(0, rows, LANES):
            energy_out[:, begin:begin + LANES] = jnp.sum(energy[pl.ds(begin, LANES), :].T, axis=0, keepdims=True)


def join(y, v, carry, states, weights, params):
    rows, chans = y.shape
    wide = math.gcd(chans, JOIN_STRIP)
    column = lambda height: pl.BlockSpec((height, wide), lambda i: (0, i))
    return pl.pallas_call(
        join_kernel,
        grid=(chans // wide,),
        out_shape=(jax.ShapeDtypeStruct((rows, chans), BF16), jax.ShapeDtypeStruct((1, rows), F32)),
        in_specs=[column(rows), column(rows), column(carry.shape[0]), pl.BlockSpec((states.shape[0], GROUP_CH, wide), lambda i: (0, 0, i)),
                  column(weights.shape[0]), column(params.shape[0])],
        out_specs=(column(rows), pl.BlockSpec((1, rows), lambda i: (0, 0))),
        scratch_shapes=[pltpu.VMEM((rows, LANES), F32)],
        compiler_params=pltpu.CompilerParams(vmem_limit_bytes=JOIN_VMEM),
        cost_estimate=pl.CostEstimate(flops=2 * rows * chans * WIDE, bytes_accessed=6 * rows * chans, transcendentals=0),
        name="join",
    )(y, v, carry, states, weights, params)


def scale_kernel(mixed, energy, gain, out, *, width):
    rows, chans = mixed.shape
    for begin in range(0, rows, LANES):
        part = pl.ds(begin, LANES)
        scale = jnp.sum(energy[:, begin:begin + LANES], axis=0, keepdims=True)
        scale = lax.rsqrt(scale / width + 1e-06)
        scale = jnp.broadcast_to(scale, (LANES, LANES)).T
        for left in range(0, chans, LANES):
            here = slice(left, left + LANES)
            out[part, here] = (mixed[part, here].astype(F32) * scale * gain[:, here]).astype(BF16)


def scaled(mixed, energy, gain, width):
    rows, chans = mixed.shape
    tall = math.gcd(rows, 512)
    block = pl.BlockSpec((tall, chans), lambda i: (i, 0))
    return pl.pallas_call(
        functools.partial(scale_kernel, width=width),
        grid=(rows // tall,),
        out_shape=jax.ShapeDtypeStruct((rows, chans), BF16),
        in_specs=[block, pl.BlockSpec((energy.shape[0], tall), lambda i: (0, i)), pl.BlockSpec((1, chans), lambda i: (0, 0))],
        out_specs=block,
        compiler_params=pltpu.CompilerParams(vmem_limit_bytes=JOIN_VMEM),
        name="scale",
    )(mixed, energy, gain)


def local(queries, key_rows, value_rows, short_filter, medium_filter, decays, residue, skip_gain,
          norm_gain, width):
    rows, chans = queries.shape
    queries, key_rows, value_rows = (pltpu.with_memory_space_constraint(array, pltpu.HBM)
                                     for array in (queries, key_rows, value_rows))
    amplitude = residue * jnp.sqrt(-jnp.expm1(-2.0 * decays))
    params = jnp.concatenate([
        jnp.repeat(short_filter, GROUP_CH, axis=1),
        decays.reshape(1, chans), amplitude.reshape(1, chans), skip_gain[None, :],
        jnp.zeros((16 - SHORT - 3, chans), F32)], axis=0)
    halo = passed_along(edge(queries, key_rows, value_rows, pltpu.with_memory_space_constraint(short_filter, pltpu.HBM)), "context", 1)
    first, keys_t = (pltpu.with_memory_space_constraint(array, pltpu.VMEM)
                     for array in gate(queries, key_rows, value_rows, params))
    y, carry, state = mix(first, keys_t, halo, queries, key_rows, value_rows, params, medium_filter.T.astype(F32))
    states = lax.all_gather(state, "context")
    count = lax.axis_size("context")
    gap = (lax.axis_index("context") - 1 - jnp.arange(count)).astype(F32)[:, None]
    weights = jnp.where(gap >= 0.0, jnp.exp(-params[RATE:RATE + 1] * (jnp.maximum(gap, 0.0) * rows)), 0.0)
    y = pltpu.with_memory_space_constraint(y, pltpu.VMEM)
    mixed, energy = join(y, value_rows, carry, states, weights, params)
    energy = summed(energy, "tensor")
    mixed = pltpu.with_memory_space_constraint(mixed, pltpu.VMEM)
    return scaled(mixed, energy, norm_gain[None, :], width)


def solution(mesh):
    def whole(*args):
        return jax.shard_map(
            functools.partial(local, width=args[0].shape[1]),
            mesh=mesh,
            in_specs=(
                P("context", "tensor"),
                P("context", "tensor"),
                P("context", "tensor"),
                P(None, "tensor"),
                P(None, "tensor"),
                P("tensor", None),
                P("tensor", None),
                P("tensor"),
                P("tensor"),
            ),
            out_specs=P("context", "tensor"),
            check_vma=False,
        )(*args)

    return whole
```

```python
import functools
import math

import jax
import jax.numpy as jnp
from jax import lax
from jax.experimental import pallas as pl
from jax.experimental.pallas import tpu as pltpu
from jax.sharding import PartitionSpec as P

GROUP_CH = 16
LANES = 128
PACK = LANES // GROUP_CH
WIDE = 256
MODES = 16
SHORT = 7
RATE, AMP, SKIP = SHORT, SHORT + 1, SHORT + 2
GATE_STRIP = 256
MIX_STRIP = 512
EDGE_PARTS = 1
JOIN_STRIP = 512
MIX_VMEM = 24 << 20
JOIN_VMEM = 24 << 20
F32 = jnp.float32
BF16 = jnp.bfloat16


def split2(value):
    high = value.astype(BF16)
    return high, (value - high.astype(F32)).astype(BF16)


def passed_along(value, axis, steps):
    count = lax.axis_size(axis)
    return lax.ppermute(value, axis, [(source, source + steps) for source in range(count - steps)])


def edge_kernel(q, k, v, short_filter, halo_out, gated):
    rows, wide = q.shape
    begin = rows - LANES
    pack = wide // GROUP_CH
    spread = (lax.broadcasted_iota(jnp.int32, (pack, wide), 1) // GROUP_CH
              == lax.broadcasted_iota(jnp.int32, (pack, wide), 0)).astype(F32)
    taps = jnp.dot(short_filter[...], spread, precision=lax.Precision.HIGHEST, preferred_element_type=F32)
    kv = k[begin - 16:, :].astype(F32) * v[begin - 16:, :].astype(F32)
    gated[...] = kv
    total = taps[0:1, :] * gated[16:, :]
    for delay in range(1, SHORT):
        total = total + taps[delay:delay + 1, :] * gated[pl.ds(16 - delay, LANES), :]
    halo_out[0:LANES, :] = (q[begin:, :].astype(F32) * total).astype(BF16)
    last = kv[LANES + 8:, :]
    high = last.astype(BF16).astype(F32)
    halo_out[LANES:LANES + 16, :] = jnp.concatenate([high, last - high], axis=0).astype(BF16)


def edge(q, k, v, short_filter):
    rows, chans = q.shape
    wide = chans // EDGE_PARTS
    tall = math.gcd(rows, 256)
    last = pl.BlockSpec((tall, wide), lambda i: (rows // tall - 1, i))
    column = lambda height, width: pl.BlockSpec((height, width), lambda i: (0, i))
    if EDGE_PARTS > 1 and wide // GROUP_CH % LANES:
        short_filter = short_filter.reshape(SHORT, EDGE_PARTS, wide // GROUP_CH).transpose(1, 0, 2)
        tap_spec = pl.BlockSpec((pl.Squeezed(), SHORT, wide // GROUP_CH), lambda i: (i, 0, 0))
    else:
        tap_spec = column(SHORT, wide // GROUP_CH)
    return pl.pallas_call(
        edge_kernel,
        grid=(EDGE_PARTS,),
        out_shape=jax.ShapeDtypeStruct((LANES + 16, chans), BF16),
        in_specs=[last] * 3 + [tap_spec],
        out_specs=column(LANES + 16, wide),
        scratch_shapes=[pltpu.VMEM((LANES + 16, wide), F32)],
        compiler_params=pltpu.CompilerParams(vmem_limit_bytes=MIX_VMEM),
        name="edge",
    )(q, k, v, short_filter)


def gate_kernel(q, k, v, params, first_out, key_out, *gated_refs):
    rows, wide = q.shape
    for s, gated in enumerate(gated_refs):
        here = slice(s * LANES, (s + 1) * LANES)
        taps = params[:, here]
        gated[0:8, :] = jnp.zeros((8, LANES), F32)
        for begin in range(0, rows, LANES):
            part = pl.ds(begin, LANES)
            keys = k[part, here]
            fresh = keys.astype(F32) * v[part, here].astype(F32)
            gated[pl.ds(begin + 8, LANES), :] = fresh
            total = taps[0:1, :] * fresh
            for delay in range(1, SHORT):
                total = total + taps[delay:delay + 1, :] * gated[pl.ds(begin + 8 - delay, LANES), :]
            first = (q[part, here].astype(F32) * total).astype(BF16)
            first_out[here, begin:begin + LANES] = first.T
            key_out[here, begin:begin + LANES] = keys.T


def gate(q, k, v, params):
    rows, chans = q.shape
    column = lambda height: pl.BlockSpec((height, GATE_STRIP), lambda i: (0, i))
    down = pl.BlockSpec((GATE_STRIP, rows), lambda i: (i, 0))
    return pl.pallas_call(
        gate_kernel,
        grid=(chans // GATE_STRIP,),
        out_shape=(jax.ShapeDtypeStruct((chans, rows), BF16),) * 2,
        in_specs=[column(rows)] * 3 + [column(params.shape[0])],
        out_specs=(down, down),
        scratch_shapes=[pltpu.VMEM((rows + 8, LANES), F32)] * (GATE_STRIP // LANES),
        compiler_params=pltpu.CompilerParams(vmem_limit_bytes=MIX_VMEM),
        cost_estimate=pl.CostEstimate(flops=64 * rows * chans, bytes_accessed=10 * rows * chans, transcendentals=0),
        name="gate",
    )(q, k, v, params)


def summed(value, axis):
    count = lax.axis_size(axis)
    if count & (count - 1):
        return lax.psum(value, axis)
    step = 1
    while step < count:
        value = value + lax.ppermute(value, axis, [(source, source ^ step) for source in range(count)])
        step *= 2
    return value


def mix_kernel(first, keys_t, halo, q, k, v, params, medium_taps, y_out, carry_out, state_out, *scratch):
    strips = first.shape[0] // LANES
    for s in range(strips):
        here = slice(s * LANES, (s + 1) * LANES)
        mix_strip(first.at[here, :], keys_t.at[here, :], halo.at[:, here], q.at[:, here], k.at[:, here], v.at[:, here],
                  params.at[:, here], medium_taps.at[s * PACK:(s + 1) * PACK, :],
                  y_out.at[:, here], carry_out.at[:, here], state_out.at[:, here], *scratch[4 * s:4 * s + 4])


def mix_strip(first_t, key_t, halo, q, k, v, late_params, medium_taps, y_out, carry_out, state_out, y_t, seconds,
              gated, start):
    rows = first_t.shape[1]
    blocks = rows // WIDE
    halves = rows // LANES
    row_i = lax.broadcasted_iota(jnp.int32, (LANES, LANES), 0)
    col_i = lax.broadcasted_iota(jnp.int32, (LANES, LANES), 1)
    causal = col_i >= row_i
    zero = jnp.zeros((LANES, LANES), BF16)
    time_down = lax.broadcasted_iota(jnp.int32, (WIDE, LANES), 0).astype(F32)
    time_along = lax.broadcasted_iota(jnp.int32, (LANES, WIDE), 1).astype(F32)
    lane_group = lax.broadcasted_iota(jnp.int32, (WIDE, LANES), 1) // MODES
    late = late_params[...]

    gated[0:8, :] = halo[LANES:LANES + 8, :].astype(F32) + halo[LANES + 8:LANES + 16, :].astype(F32)
    gated[8:24, :] = k[...].astype(F32) * v[...].astype(F32)
    total = late[0:1, :] * gated[8:24, :]
    for delay in range(1, SHORT):
        total = total + late[delay:delay + 1, :] * gated[8 - delay:24 - delay, :]
    opening = (q[...].astype(F32) * total).astype(BF16)
    opening = jnp.concatenate([opening, jnp.zeros((LANES - 16, LANES), BF16)], axis=0).T
    start[:, 0:LANES] = halo[0:LANES, :].T
    start[:, LANES:2 * LANES] = jnp.where(col_i < 16, opening, first_t[:, 0:LANES])

    def tile(chans, b):
        if b < 1:
            return start[chans, (b + 1) * LANES:(b + 2) * LANES]
        return first_t[chans, b * LANES:(b + 1) * LANES]

    def medium_of(g):
        chans = pl.ds(g * GROUP_CH, GROUP_CH)
        turned = jnp.broadcast_to(medium_taps[g:g + 1, :], (LANES, LANES))
        turned = pltpu.roll(turned, 0, 1, stride=1, stride_axis=0)
        medium_w = jnp.concatenate(
            [jnp.where(causal, 0.0, turned), jnp.where(causal, turned, 0.0)], axis=0).astype(BF16)
        window = jnp.concatenate([jnp.concatenate([tile(chans, b - 1), tile(chans, b)], axis=1) for b in range(halves)], axis=0)
        medium = jnp.dot(window, medium_w, preferred_element_type=F32)
        key = jnp.concatenate([key_t[chans, b * LANES:(b + 1) * LANES] for b in range(halves)], axis=0)
        second = (key.astype(F32) * medium).astype(BF16)
        for b in range(halves):
            seconds[(b // 2) * GROUP_CH:(b // 2 + 1) * GROUP_CH,
                    g * WIDE + (b % 2) * LANES:g * WIDE + (b % 2 + 1) * LANES] = (
                second[b * GROUP_CH:(b + 1) * GROUP_CH])

    for g in range(PACK):
        medium_of(g)

    rate = late[RATE:RATE + 1, :]
    tails = jnp.exp(-rate * (WIDE - 1.0 - time_down)).astype(BF16)
    tails_w = jnp.concatenate([jnp.where(lane_group == g, tails, jnp.zeros_like(tails)) for g in range(PACK)], axis=0)
    sums = jnp.dot(seconds[...], tails_w, preferred_element_type=F32)
    decay = jnp.exp(-rate * float(WIDE))
    state = jnp.zeros((GROUP_CH, LANES), F32)
    for b in range(blocks):
        carry_out[b * GROUP_CH:(b + 1) * GROUP_CH, :] = state
        state = decay * state + sums[b * GROUP_CH:(b + 1) * GROUP_CH, :]
    state_out[...] = state.astype(BF16)

    down = lambda row: jnp.broadcast_to(late[row:row + 1, :], (LANES, LANES)).T
    rate_t, amp_t, skip_t = down(RATE), down(AMP), down(SKIP)
    both = lambda half: jnp.concatenate([half, half], axis=1)
    power = both(amp_t) * jnp.exp(-both(rate_t) * time_along)

    def long_of(g):
        chans = pl.ds(g * GROUP_CH, GROUP_CH)
        mine = slice(g * MODES, (g + 1) * MODES)
        profile = jnp.sum(power[mine], axis=0, keepdims=True)
        soon, late_part = (
            pltpu.roll(jnp.broadcast_to(profile[:, half * LANES:(half + 1) * LANES], (LANES, LANES)),
                       0, 1, stride=1, stride_axis=0) for half in range(2))
        near = jnp.where(causal, soon, 0.0).astype(BF16)
        far = jnp.where(causal, late_part, soon).astype(BF16)
        pieces = [jnp.concatenate([near, far], axis=1), jnp.concatenate([zero, near], axis=1)]
        second = seconds[:, g * WIDE:(g + 1) * WIDE]
        y = jnp.dot(second, jnp.concatenate(pieces, axis=0), preferred_element_type=F32)
        gain = both(skip_t[g * GROUP_CH:(g + 1) * GROUP_CH, :])
        gain = jnp.concatenate([gain] * blocks, axis=0)
        y = (y + gain * second.astype(F32)).astype(BF16)
        for b in range(blocks):
            y_t[chans, b * WIDE:(b + 1) * WIDE] = y[b * GROUP_CH:(b + 1) * GROUP_CH, :]

    for g in range(PACK):
        long_of(g)
    for begin in range(0, rows, LANES):
        y_out[pl.ds(begin, LANES), :] = y_t[:, begin:begin + LANES].T


def mix(first, keys_t, halo, q, k, v, params, medium_taps):
    chans, rows = first.shape
    column = lambda height: pl.BlockSpec((height, MIX_STRIP), lambda i: (0, i))
    down = lambda height, width: pl.BlockSpec((height, width), lambda i: (i, 0))
    carried = rows // WIDE * GROUP_CH
    return pl.pallas_call(
        mix_kernel,
        grid=(chans // MIX_STRIP,),
        out_shape=(jax.ShapeDtypeStruct((rows, chans), BF16), jax.ShapeDtypeStruct((carried, chans), F32),
                   jax.ShapeDtypeStruct((GROUP_CH, chans), BF16)),
        in_specs=[down(MIX_STRIP, rows)] * 2 + [column(halo.shape[0])] + [column(16)] * 3 + [
            column(params.shape[0]), down(MIX_STRIP // GROUP_CH, LANES)],
        out_specs=(column(rows), column(carried), column(GROUP_CH)),
        scratch_shapes=[
            pltpu.VMEM((LANES, rows), BF16),
            pltpu.VMEM((LANES, PACK * WIDE), BF16),
            pltpu.VMEM((24, LANES), F32),
            pltpu.VMEM((LANES, 2 * LANES), BF16),
        ] * (MIX_STRIP // LANES),
        compiler_params=pltpu.CompilerParams(vmem_limit_bytes=JOIN_VMEM),
        cost_estimate=pl.CostEstimate(flops=8 * rows * chans * WIDE, bytes_accessed=6 * rows * chans, transcendentals=0),
        name="mix",
    )(first, keys_t, halo, q, k, v, params, medium_taps)


def join_kernel(y, v, carry, states, weights, params, mixed_out, energy_out, energy, *leads):
    rows, wide = y.shape
    step = pl.program_id(0)

    @pl.when(step == 0)
    def _():
        energy[...] = jnp.zeros_like(energy)

    own = (lax.broadcasted_iota(jnp.int32, (WIDE, WIDE), 0) // GROUP_CH
           == lax.broadcasted_iota(jnp.int32, (WIDE, WIDE), 1) // MODES)
    time = lax.broadcasted_iota(jnp.int32, (WIDE, WIDE), 0).astype(F32) + 1.0
    nothing = jnp.zeros((WIDE, WIDE), BF16)
    entry = jnp.zeros((GROUP_CH, wide), F32)
    for source in range(states.shape[0]):
        entry = entry + weights[source:source + 1, :] * states[source].astype(F32)
    pieces = [slice(s * WIDE, (s + 1) * WIDE) for s in range(wide // WIDE)]
    rates = [params[RATE:RATE + 1, here] for here in pieces]
    for here, rate, lead in zip(pieces, rates, leads):
        lead[...] = (params[AMP:AMP + 1, here] * jnp.exp(-rate * time)).astype(BF16)
    for b in range(rows // WIDE):
        part = pl.ds(b * WIDE, WIDE)
        total = energy[part, :]
        for here, rate, lead in zip(pieces, rates, leads):
            state = carry[b * GROUP_CH:(b + 1) * GROUP_CH, here] + jnp.exp(-rate * float(b * WIDE)) * entry[:, here]
            spread = jnp.concatenate([state.astype(BF16)] * (WIDE // GROUP_CH), axis=0)
            carried = lax.dot_general(lead[...], jnp.where(own, spread, nothing), (((1,), (1,)), ((), ())),
                                      preferred_element_type=F32)
            mixed = v[part, here].astype(F32) * (y[part, here].astype(F32) + carried)
            mixed_out[part, here] = mixed.astype(BF16)
            square = mixed * mixed
            total = total + square[:, :LANES] + square[:, LANES:]
        energy[part, :] = total

    @pl.when(step == pl.num_programs(0) - 1)
    def _():
        for begin in range(0, rows, LANES):
            energy_out[:, begin:begin + LANES] = jnp.sum(energy[pl.ds(begin, LANES), :].T, axis=0, keepdims=True)


def join(y, v, carry, states, weights, params):
    rows, chans = y.shape
    wide = math.gcd(chans, JOIN_STRIP)
    column = lambda height: pl.BlockSpec((height, wide), lambda i: (0, i))
    return pl.pallas_call(
        join_kernel,
        grid=(chans // wide,),
        out_shape=(jax.ShapeDtypeStruct((rows, chans), BF16), jax.ShapeDtypeStruct((1, rows), F32)),
        in_specs=[column(rows), column(rows), column(carry.shape[0]), pl.BlockSpec((states.shape[0], GROUP_CH, wide), lambda i: (0, 0, i)),
                  column(weights.shape[0]), column(params.shape[0])],
        out_specs=(column(rows), pl.BlockSpec((1, rows), lambda i: (0, 0))),
        scratch_shapes=[pltpu.VMEM((rows, LANES), F32)] + [pltpu.VMEM((WIDE, WIDE), BF16)] * (wide // WIDE),
        compiler_params=pltpu.CompilerParams(vmem_limit_bytes=JOIN_VMEM),
        cost_estimate=pl.CostEstimate(flops=2 * rows * chans * WIDE, bytes_accessed=6 * rows * chans, transcendentals=0),
        name="join",
    )(y, v, carry, states, weights, params)


def scale_kernel(mixed, energy, gain, out, *, width):
    rows, chans = mixed.shape
    for begin in range(0, rows, LANES):
        part = pl.ds(begin, LANES)
        scale = jnp.sum(energy[:, begin:begin + LANES], axis=0, keepdims=True)
        scale = lax.rsqrt(scale / width + 1e-06)
        scale = jnp.broadcast_to(scale, (LANES, LANES)).T
        for left in range(0, chans, LANES):
            here = slice(left, left + LANES)
            out[part, here] = (mixed[part, here].astype(F32) * scale * gain[:, here]).astype(BF16)


def scaled(mixed, energy, gain, width):
    rows, chans = mixed.shape
    tall = math.gcd(rows, 512)
    block = pl.BlockSpec((tall, chans), lambda i: (i, 0))
    return pl.pallas_call(
        functools.partial(scale_kernel, width=width),
        grid=(rows // tall,),
        out_shape=jax.ShapeDtypeStruct((rows, chans), BF16),
        in_specs=[block, pl.BlockSpec((energy.shape[0], tall), lambda i: (0, i)), pl.BlockSpec((1, chans), lambda i: (0, 0))],
        out_specs=block,
        compiler_params=pltpu.CompilerParams(vmem_limit_bytes=JOIN_VMEM),
        name="scale",
    )(mixed, energy, gain)


def local(queries, key_rows, value_rows, short_filter, medium_filter, decays, residue, skip_gain,
          norm_gain, width):
    rows, chans = queries.shape
    queries, key_rows, value_rows = (pltpu.with_memory_space_constraint(array, pltpu.HBM)
                                     for array in (queries, key_rows, value_rows))
    amplitude = residue * jnp.sqrt(-jnp.expm1(-2.0 * decays))
    params = jnp.concatenate([
        jnp.repeat(short_filter, GROUP_CH, axis=1),
        decays.reshape(1, chans), amplitude.reshape(1, chans), skip_gain[None, :],
        jnp.zeros((16 - SHORT - 3, chans), F32)], axis=0)
    halo = passed_along(edge(queries, key_rows, value_rows, pltpu.with_memory_space_constraint(short_filter, pltpu.HBM)), "context", 1)
    first, keys_t = (pltpu.with_memory_space_constraint(array, pltpu.VMEM)
                     for array in gate(queries, key_rows, value_rows, params))
    y, carry, state = mix(first, keys_t, halo, queries, key_rows, value_rows, params, medium_filter.T.astype(F32))
    states = lax.all_gather(state, "context")
    count = lax.axis_size("context")
    gap = (lax.axis_index("context") - 1 - jnp.arange(count)).astype(F32)[:, None]
    weights = jnp.where(gap >= 0.0, jnp.exp(-params[RATE:RATE + 1] * (jnp.maximum(gap, 0.0) * rows)), 0.0)
    y = pltpu.with_memory_space_constraint(y, pltpu.VMEM)
    mixed, energy = join(y, value_rows, carry, states, weights, params)
    energy = summed(energy, "tensor")
    mixed = pltpu.with_memory_space_constraint(mixed, pltpu.VMEM)
    return scaled(mixed, energy, norm_gain[None, :], width)


def solution(mesh):
    def whole(*args):
        return jax.shard_map(
            functools.partial(local, width=args[0].shape[1]),
            mesh=mesh,
            in_specs=(
                P("context", "tensor"),
                P("context", "tensor"),
                P("context", "tensor"),
                P(None, "tensor"),
                P(None, "tensor"),
                P("tensor", None),
                P("tensor", None),
                P("tensor"),
                P("tensor"),
            ),
            out_specs=P("context", "tensor"),
            check_vma=False,
        )(*args)

    return whole
```
